32 devices in a mesh: seq: 32 (over z, y, x, core), head: 1.
Axes of the slice: x: 2, y: 2, z: 4, core: 2. Of those that a mesh axis runs over, the one named last changes fastest.
Arguments:
- video: bfloat16 [8192, 3072], P('seq'), may hold values from -6 to 6
- cotangent: bfloat16 [8192, 3072], P('seq'), may hold values from -48 to 48
- text_embed: bfloat16 [256, 4096], P(None, 'seq'), may hold values from -700 to 700
- text_gain: float32 [4096], P('seq'), may hold values from 0.25 to 1.75
- w_query: bfloat16 [3072, 3072], P('seq', 'head'), may hold values from -0.109375 to 0.109375
- w_key: bfloat16 [4096, 3072], P('seq', 'head'), may hold values from -0.09375 to 0.09375
- w_value: bfloat16 [4096, 3072], P('seq', 'head'), may hold values from -0.09375 to 0.09375
- w_out: bfloat16 [3072, 3072], P('head', 'seq'), may hold values from -0.109375 to 0.109375
Outputs:
- grad_video: bfloat16 [8192, 3072], P('seq', 'head')
- grad_text: float32 [256, 4096], P(None, 'seq')
The draws below stay inside these ranges and needn't reach their ends.
All inputs are finite; a program needn't handle non-finite values.
Results may differ from the reference program's by a relative error of at most 0.012.
Values may be sent and summed in bfloat16 or wider, within the bound.
A program may use at most 128 MiB of HBM per device.

```python
import jax
import jax.numpy as jnp
from jax import lax

D = 3072
HEADS = 24
HEAD_DIM = 128
TEXT_LEN = 256
TEXT_DIM = 4096
TOKENS = 8192


def draw_text_embed(key, part):
    key_rows, key_cols, key_main = jax.random.split(key, 3)
    row_scale = 10.0 ** jax.random.uniform(key_rows, (TEXT_LEN, 1), jnp.float32)
    column = jnp.arange(TEXT_DIM, dtype=jnp.float32)
    trend = jnp.sqrt(1.0 + 2.0 * column / max(TEXT_DIM - 1, 1))
    col_scale = 10.0 ** jax.random.uniform(key_cols, (1, TEXT_DIM), jnp.float32) * trend[None, :]
    entries = jnp.clip(jax.random.normal(key_main, (TEXT_LEN, TEXT_DIM), jnp.float32), -4.0, 4.0)
    return (entries * row_scale * col_scale).astype(jnp.bfloat16)


def level_of(stream_key, extent, shards, smallest, high):
    level, own = 1.0, jax.random.fold_in(stream_key, 6)
    for position, blocks in shards:
        steps = jnp.exp(jax.random.uniform(jax.random.fold_in(own, position), (blocks,), jnp.float32, smallest / len(shards), high / len(shards)))
        level = level * jnp.repeat(steps, extent[position] // blocks).reshape([-1 if axis == position else 1 for axis in range(len(extent))])
    return level


def gaussian(rng, extent, width, most, cuts=(), kind=jnp.bfloat16):
    drawn = jax.random.normal(rng, extent, jnp.float32) * width
    if len(cuts) > 0:
        drawn = level_of(rng, extent, cuts, -0.22, 0.18) * drawn
    return jnp.clip(drawn, min=-most, max=most).astype(kind)


def setup_inputs(seed: int = 0) -> dict:
    arg_keys = jax.random.split(jax.random.key(seed), 9)
    return {
        "video": gaussian(arg_keys[0], (TOKENS, D), 1.0, 6.0, ((0, 32),)),
        "cotangent": gaussian(arg_keys[1], (TOKENS, D), 8.0, 48.0, ((0, 32),)),
        "text_embed": draw_text_embed(jax.random.fold_in(arg_keys[8], 71), 0),
        "text_gain": jnp.clip(1.0 + 0.15 * jax.random.normal(arg_keys[3], (TEXT_DIM,), jnp.float32), 0.25, 1.75),
        "w_query": gaussian(arg_keys[4], (D, HEADS * HEAD_DIM), D ** -0.5, 0.109375, ((0, 32),)),
        "w_key": gaussian(arg_keys[5], (TEXT_DIM, HEADS * HEAD_DIM), TEXT_DIM ** -0.5, 0.09375, ((0, 32),)),
        "w_value": gaussian(arg_keys[6], (TEXT_DIM, HEADS * HEAD_DIM), TEXT_DIM ** -0.5, 0.09375, ((0, 32),)),
        "w_out": gaussian(arg_keys[7], (HEADS * HEAD_DIM, D), (HEADS * HEAD_DIM) ** -0.5, 0.109375, ((1, 32),)),
    }


epsilon = 1e-06

def one_head(operands):
    query_head, key_head, value_head, grad_head = operands
    score_scale = HEAD_DIM ** (-0.5)
    scores = jnp.dot(query_head, key_head.T, preferred_element_type=jnp.float32) * score_scale
    raised = jnp.exp(scores)
    softmax_out = raised / lax.optimization_barrier(jnp.sum(raised, axis=1, keepdims=True))
    grad_probs = jnp.dot(grad_head, value_head.T, preferred_element_type=jnp.float32)
    row_delta = lax.optimization_barrier(jnp.sum(grad_probs * softmax_out, axis=1, keepdims=True))
    grad_scores = (softmax_out * (grad_probs - row_delta) * score_scale).astype(jnp.bfloat16)
    grad_query = jnp.dot(grad_scores, key_head, preferred_element_type=jnp.float32).astype(jnp.bfloat16)
    grad_key = jnp.dot(grad_scores.T, query_head, preferred_element_type=jnp.float32)
    grad_value = jnp.dot(softmax_out.astype(jnp.bfloat16).T, grad_head, preferred_element_type=jnp.float32)
    return (grad_query, grad_key, grad_value)

def by_heads(matrix, count):
    return matrix.reshape(count, HEADS, HEAD_DIM).transpose(1, 0, 2)

def from_heads(stacked, count):
    return stacked.transpose(1, 0, 2).reshape(count, HEADS * HEAD_DIM)

def reference(video, cotangent, text_embed, text_gain, w_query, w_key, w_value, w_out):
    contract = (((1,), (1,)), ((), ()))
    text_wide = text_embed.astype(jnp.float32)
    inverse_rms = lax.rsqrt(lax.optimization_barrier(jnp.sum(text_wide * text_wide, axis=1, keepdims=True)) / TEXT_DIM + epsilon)
    scaled_text = (text_wide * text_gain).astype(jnp.bfloat16)
    keys = (inverse_rms * jnp.dot(scaled_text, w_key, preferred_element_type=jnp.float32)).astype(jnp.bfloat16)
    text_values = (inverse_rms * jnp.dot(scaled_text, w_value, preferred_element_type=jnp.float32)).astype(jnp.bfloat16)
    query = jnp.dot(video, w_query, preferred_element_type=jnp.float32).astype(jnp.bfloat16)
    grad_out = lax.dot_general(cotangent, w_out, contract, preferred_element_type=jnp.float32).astype(jnp.bfloat16)
    grad_query, grad_keys, grad_values = lax.map(one_head, (by_heads(query, TOKENS), by_heads(keys, TEXT_LEN), by_heads(text_values, TEXT_LEN), by_heads(grad_out, TOKENS)))
    grad_query = from_heads(grad_query, TOKENS)
    grad_video = lax.dot_general(grad_query, w_query, contract, preferred_element_type=jnp.float32).astype(jnp.bfloat16)
    keys_low = from_heads(grad_keys, TEXT_LEN).astype(jnp.bfloat16)
    values_low = from_heads(grad_values, TEXT_LEN).astype(jnp.bfloat16)
    grad_normed = lax.dot_general(keys_low, w_key, contract, preferred_element_type=jnp.float32) + lax.dot_general(values_low, w_value, contract, preferred_element_type=jnp.float32)
    normed = text_wide * inverse_rms
    row_stat = lax.optimization_barrier(jnp.sum(grad_normed * text_gain * normed, axis=1, keepdims=True))
    grad_text = inverse_rms * (grad_normed * text_gain - normed * (row_stat / TEXT_DIM))
    return (grad_video, grad_text)
```

```python
import functools
import math

import jax
import jax.numpy as jnp
from jax import lax
from jax.experimental import pallas as pl
from jax.experimental.pallas import tpu as pltpu
from jax.sharding import PartitionSpec as P

HEAD_DIM = 128
ROWS = 16
MESH = pl.DeviceIdType.MESH
epsilon = 1e-06
F32 = jnp.float32
BF16 = jnp.bfloat16


def dot(a, b, dims):
    return lax.dot_general(a, b, ((dims[0:1], dims[1:2]), ((), ())), preferred_element_type=F32)


def kernel(
    n, text_dim, scaled, squares, w_key, w_value, w_query, w_out, video, cotangent,
    grad_video, grad_normed, row_stat, inverse,
    wq, wo, vid, cot, wk, wv, st, sq, sq_in,
    sums, halves, keys, grads, ghalves, gfull, query, gout, gquery, gv_send, gv_recv, gv_own, tail_send, tail_recv,
    pair_send, pair_recv, local_sem, w_send, w_recv, sq_send, sq_recv, k_send, k_recv, g_send, g_recv, end_send, end_recv,
):
    me = lax.axis_index("seq")
    chip, core = me // 2, me % 2
    other = 1 - core
    sibling = me + 1 - 2 * core
    n_bits = int(math.log2(n // 2))
    bit = [(chip // (1 << b)) % 2 for b in range(n_bits)]
    partner = [me + (1 - 2 * bit[b]) * (2 << b) for b in range(n_bits)]
    low = list(range(min(2, n_bits)))
    high = list(range(2, n_bits))
    gather_order = [high + low, high + low[::-1]]
    reduce_order = [low + high, low[::-1] + high]
    width = wq.shape[2]
    toks = vid.shape[1]
    pending = []

    barrier = pltpu.get_barrier_semaphore()
    for peer in [sibling] + partner:
        pl.semaphore_signal(barrier, inc=1, device_id={"seq": peer}, device_id_type=MESH)
    pl.semaphore_wait(barrier, 1 + n_bits)

    def send(src, dst, send_sem, recv_sem, peer):
        copy = pltpu.make_async_remote_copy(
            src_ref=src, dst_ref=dst, send_sem=send_sem, recv_sem=recv_sem,
            device_id={"seq": peer}, device_id_type=MESH,
        )
        copy.start()
        pending.append(copy)
        return copy

    mine = pl.ds(pl.multiple_of(core * width, 128), width)
    theirs = pl.ds(pl.multiple_of(other * width, 128), width)
    plan = [
        (scaled, scaled, st.at[core]),
        (w_key.at[:, mine], w_key.at[:, theirs], wk.at[core]),
        (w_value.at[:, mine], w_value.at[:, theirs], wv.at[core]),
        (squares, squares, sq.at[core]),
        (w_query.at[:, mine], w_query.at[:, theirs], wq.at[me]),
        (w_out.at[:, mine], w_out.at[:, theirs], wo.at[me]),
        (video, video, vid.at[core]),
        (cotangent, cotangent, cot.at[core]),
    ]
    shared = []
    for i, (own, away, dst) in enumerate(plan):
        remote = send(away, dst, pair_send.at[i], pair_recv.at[i], sibling)
        local = pltpu.make_async_copy(own, dst, local_sem.at[i])
        local.start()
        shared.append((remote, local))

    def have(i):
        shared[i][0].wait_recv()
        shared[i][1].wait()

    arrivals = {}

    def weights(array, buffer, p):
        for stream in range(2):
            order = gather_order[stream]
            where = chip
            for t in range(n_bits):
                if (p >> t) & 1:
                    where = where + (1 - 2 * bit[order[t]]) * (1 << order[t])
            block = buffer.at[2 * where + stream]
            if p > 0:
                arrivals[array, stream, p].wait_recv()
            for t in range(p.bit_length(), n_bits):
                q = p + (1 << t)
                arrivals[array, stream, q] = send(
                    block, block, w_send.at[array, stream, q], w_recv.at[array, stream, q], partner[order[t]]
                )

    def reduce_gather(parts, landing, full, send_sem, recv_sem, finish):
        held = parts.shape[1]
        base = [0, 0]
        sizes, bases = [], []
        offset = 0
        for step in range(n_bits):
            half = max(held // 2, 1)
            sent = []
            for i in range(2):
                b = reduce_order[i][step]
                if held > 1:
                    away = base[i] + (1 - bit[b]) * half
                    base[i] = base[i] + bit[b] * half
                else:
                    away = base[i]
                sent.append(
                    send(
                        parts.at[i, pl.ds(away, half)], landing.at[i, pl.ds(offset, half)],
                        send_sem.at[i, step], recv_sem.at[i, step], partner[b],
                    )
                )
            yield
            for i in range(2):
                sent[i].wait_recv()
                if held == 1:
                    sent[i].wait_send()
                    pending[:] = [copy for copy in pending if copy is not sent[i]]
                spot = pl.ds(base[i], half)
                total = parts[i, spot].astype(F32) + landing[i, offset : offset + half].astype(F32)
                parts[i, spot] = total.astype(BF16)
            sizes.append((step, half) if held > 1 else None)
            bases.append(list(base))
            offset += half
            held = half
        for i in range(2):
            finish(i, base[i], held)
        for entry in range(n_bits - 1, -1, -1):
            if sizes[entry] is None:
                continue
            step, half = sizes[entry]
            sent = []
            for i in range(2):
                spot = full.at[i, pl.ds(bases[entry][i], half)]
                sent.append(
                    send(
                        spot, spot, send_sem.at[i, n_bits + step], recv_sem.at[i, n_bits + step],
                        partner[reduce_order[i][step]],
                    )
                )
            yield
            for i in range(2):
                sent[i].wait_recv()

    def square_sum():
        have(3)
        sq_in[0] = sq[0] + sq[1]
        for b in range(n_bits):
            copy = send(sq_in.at[b], sq.at[2 + b], sq_send.at[b], sq_recv.at[b], partner[b])
            yield
            copy.wait_recv()
            sq_in[b + 1] = sq_in[b] + sq[2 + b]
        inverse[...] = lax.rsqrt(sq_in[n_bits] / text_dim + epsilon)

    def drain(generator, steps=None):
        count = 0
        for _ in generator:
            count += 1
            if steps is not None and count >= steps:
                return

    pieces = sums.shape[1]
    for i in range(3):
        have(i)
    for i, w in ((0, wk), (1, wv)):
        part = dot(st[0], w[0], (1, 0)) + dot(st[1], w[1], (1, 0))
        sums[i] = part.astype(BF16).reshape(pieces, ROWS, width)

    def finish_keys(i, base, held):
        inv = inverse[pl.ds(pl.multiple_of(base * ROWS, ROWS), held * ROWS), :][:, 0:1]
        total = sums[i, pl.ds(base, held)].astype(F32).reshape(held * ROWS, width)
        keys[i, pl.ds(base, held)] = (inv * total).astype(BF16).reshape(held, ROWS, width)

    text_sum = reduce_gather(sums, halves, keys, k_send, k_recv, finish_keys)
    norm_sum = square_sum()
    next(text_sum)
    next(norm_sum)
    have(4)
    weights(0, wq, 0)
    have(5)
    weights(1, wo, 0)
    blocks = 1 << n_bits
    near = blocks // 2
    small = [(0, wq, p) for p in range(1, near)] + [(1, wo, p) for p in range(1, near)]
    for i, event in enumerate(small):
        weights(*event)
        drain(norm_sum, 1)
        if i >= 1:
            drain(text_sum, 1)
    drain(norm_sum)
    drain(text_sum)
    for p in range(near, blocks):
        weights(0, wq, p)
    have(6)
    tile = 256 if width % 256 == 0 else 128

    def project(rows, w, out):
        def body(t, _):
            cols = pl.ds(pl.multiple_of(t * tile, tile), tile)
            wide = w[:, :, cols].reshape(-1, tile)
            out[:, cols] = dot(rows[...].reshape(2 * toks, -1), wide, (1, 0)).astype(BF16)
            return 0

        lax.fori_loop(0, width // tile, body, 0)

    project(vid, wq, query)
    for p in range(near, blocks):
        weights(1, wo, p)
    have(7)
    project(cot, wo, gout)

    scale = HEAD_DIM ** (-0.5)
    text_len = pieces * ROWS

    def attention(h, _):
        cols = pl.ds(pl.multiple_of(h * HEAD_DIM, HEAD_DIM), HEAD_DIM)
        key = keys[0, :, :, cols].reshape(text_len, HEAD_DIM)
        value = keys[1, :, :, cols].reshape(text_len, HEAD_DIM)
        q, g = query[:, cols], gout[:, cols]
        raised = jnp.exp(dot(key, q, (1, 1)) * scale)
        probs = raised / jnp.sum(raised, axis=0, keepdims=True)
        grad_probs = dot(value, g, (1, 1))
        delta = jnp.sum(grad_probs * probs, axis=0, keepdims=True)
        grad_scores = (probs * (grad_probs - delta) * scale).astype(BF16)
        gquery[:, cols] = dot(grad_scores, key, (0, 0)).astype(BF16)
        grads[0, :, :, cols] = dot(grad_scores, q, (1, 0)).astype(BF16).reshape(pieces, ROWS, HEAD_DIM)
        grads[1, :, :, cols] = dot(probs.astype(BF16), g, (1, 0)).astype(BF16).reshape(pieces, ROWS, HEAD_DIM)
        return 0

    lax.fori_loop(0, width // HEAD_DIM, attention, 0)

    def finish_grads(i, base, held):
        gfull[i, pl.ds(base, held)] = grads[i, pl.ds(base, held)]

    grad_sum = reduce_gather(grads, ghalves, gfull, g_send, g_recv, finish_grads)
    next(grad_sum)
    span = 8 * wq.shape[1]

    def back(rows, first, last, out):
        def body(t, _):
            wide = wq[pl.ds(t * 8, 8)].reshape(span, width)
            cols = pl.ds(pl.multiple_of(t * span, 128), span)
            left = gquery[pl.ds(pl.multiple_of(rows * toks, toks), toks), :]
            out[:, cols] = dot(left, wide, (1, 1)).astype(out.dtype)
            return 0

        lax.fori_loop(first, last, body, 0)

    tiles = n // 8
    back(other, 0, tiles // 2, gv_send)
    drain(grad_sum, 1)
    back(other, tiles // 2, tiles, gv_send)
    gv_copy = send(gv_send, gv_recv, end_send.at[0], end_recv.at[0], sibling)
    drain(grad_sum, 1)
    for t in range(tiles):
        back(core, t, t + 1, gv_own)
        drain(grad_sum, 1)
    gv_copy.wait_recv()
    grad_video[...] = (gv_own[...] + gv_recv[...].astype(F32)).astype(BF16)
    drain(grad_sum)

    gk, gv = gfull[0].reshape(text_len, width), gfull[1].reshape(text_len, width)
    tail_send[0] = dot(gk, wk[other], (1, 1)) + dot(gv, wv[other], (1, 1))
    stat = jnp.sum(
        gk.astype(F32) * keys[0].reshape(text_len, width).astype(F32)
        + gv.astype(F32) * keys[1].reshape(text_len, width).astype(F32),
        axis=1, keepdims=True,
    )
    tail_send[1] = jnp.broadcast_to(stat, tail_send.shape[1:])
    last = send(tail_send, tail_recv, end_send.at[1], end_recv.at[1], sibling)
    own = dot(gk, wk[core], (1, 1)) + dot(gv, wv[core], (1, 1))
    last.wait_recv()
    grad_normed[...] = own + tail_recv[0]
    row_stat[...] = (tail_send[1] + tail_recv[1])[:, 0:128]
    for copy in pending:
        copy.wait_send()


def body(n, heads_split, text_dim, video, cotangent, text_embed, text_gain, w_query, w_key, w_value, w_out):
    toks, model = video.shape
    text_len, feats = text_embed.shape
    rows = w_query.shape[0]
    width = w_query.shape[1] // 2
    n_bits = int(math.log2(n // 2))
    pieces = text_len // ROWS
    text_wide = text_embed.astype(F32)
    scaled = (text_wide * text_gain).astype(BF16)
    squares = jnp.broadcast_to(jnp.sum(text_wide * text_wide, axis=1, keepdims=True), (text_len, 128))
    lanes = -(-feats // 128) * 128
    if lanes > feats:
        scaled = jnp.pad(scaled, ((0, 0), (0, lanes - feats)))
        w_key, w_value = (jnp.pad(w, ((0, lanes - feats), (0, 0))) for w in (w_key, w_value))
    vmem, dma = pltpu.VMEM, pltpu.SemaphoreType.DMA
    landing = pieces + n_bits
    side = 2 * toks
    flops = 6 * side * model * width + 10 * side * text_len * width
    out = pl.pallas_call(
        functools.partial(kernel, n, text_dim),
        out_shape=[
            jax.ShapeDtypeStruct((toks, model), BF16),
            jax.ShapeDtypeStruct((text_len, lanes), F32),
            jax.ShapeDtypeStruct((text_len, 128), F32),
            jax.ShapeDtypeStruct((text_len, 128), F32),
        ],
        in_specs=[pl.BlockSpec(memory_space=pl.ANY)] * 8,
        out_specs=[pl.BlockSpec(memory_space=pltpu.VMEM)] * 4,
        scratch_shapes=[
            vmem((n, rows, width), BF16),
            vmem((n, rows, width), BF16),
            vmem((2, toks, model), BF16),
            vmem((2, toks, model), BF16),
            vmem((2, lanes, width), BF16),
            vmem((2, lanes, width), BF16),
            vmem((2, text_len, lanes), BF16),
            vmem((2 + n_bits, text_len, 128), F32),
            vmem((1 + n_bits, text_len, 128), F32),
            vmem((2, pieces, ROWS, width), BF16),
            vmem((2, landing, ROWS, width), BF16),
            vmem((2, pieces, ROWS, width), BF16),
            vmem((2, pieces, ROWS, width), BF16),
            vmem((2, landing, ROWS, width), BF16),
            vmem((2, pieces, ROWS, width), BF16),
            vmem((side, width), BF16),
            vmem((side, width), BF16),
            vmem((side, width), BF16),
            vmem((toks, model), BF16),
            vmem((toks, model), BF16),
            vmem((toks, model), F32),
            vmem((2, text_len, lanes), F32),
            vmem((2, text_len, lanes), F32),
            dma((8,)),
            dma((8,)),
            dma((8,)),
            dma((2, 2, n // 2)),
            dma((2, 2, n // 2)),
            dma((n_bits,)),
            dma((n_bits,)),
            dma((2, 2 * n_bits)),
            dma((2, 2 * n_bits)),
            dma((2, 2 * n_bits)),
            dma((2, 2 * n_bits)),
            dma((2,)),
            dma((2,)),
        ],
        compiler_params=pltpu.CompilerParams(
            collective_id=0, has_side_effects=True, vmem_limit_bytes=60 * 1024 * 1024
        ),
        cost_estimate=pl.CostEstimate(
            flops=flops, bytes_accessed=8 * toks * model, transcendentals=side * text_len * width // HEAD_DIM
        ),
    )(scaled, squares, w_key, w_value, w_query, w_out.T, video, cotangent)
    grad_video, grad_normed, row_stat, inverse = out
    grad_normed = grad_normed[:, 0:feats]
    if heads_split > 1:
        grad_normed, row_stat = lax.psum((grad_normed, row_stat), "head")
        grad_video = lax.psum_scatter(grad_video, "head", scatter_dimension=1, tiled=True)
    inv = inverse[:, 0:1]
    grad_text = inv * (grad_normed * text_gain - text_wide * inv * (row_stat[:, 0:1] / text_dim))
    return (grad_video, grad_text)


def solution(mesh):
    n, heads_split = mesh.shape["seq"], mesh.shape["head"]
    in_specs = (
        P("seq", None),
        P("seq", None),
        P(None, "seq"),
        P("seq"),
        P("seq", "head"),
        P("seq", "head"),
        P("seq", "head"),
        P("head", "seq"),
    )
    out_specs = (P("seq", "head"), P(None, "seq"))

    def whole(video, cotangent, text_embed, *rest):
        run = functools.partial(body, n, heads_split, text_embed.shape[1])
        mapped = jax.shard_map(run, mesh=mesh, in_specs=in_specs, out_specs=out_specs, check_vma=False)
        return mapped(video, cotangent, text_embed, *rest)

    return whole
```

```python
import functools
import math

import jax
import jax.numpy as jnp
from jax import lax
from jax.experimental import pallas as pl
from jax.experimental.pallas import tpu as pltpu
from jax.sharding import PartitionSpec as P

HEAD_DIM = 128
ROWS = 16
MESH = pl.DeviceIdType.MESH
epsilon = 1e-06
F32 = jnp.float32
BF16 = jnp.bfloat16


def dot(a, b, dims):
    return lax.dot_general(a, b, ((dims[0:1], dims[1:2]), ((), ())), preferred_element_type=F32)


def kernel(
    n, size, text_dim, scaled, squares, w_key, w_value, w_query, w_out, video, cotangent,
    grad_video, grad_normed, row_stat, inverse,
    wq, wo, vid, cot, wk, wv, st, sq, sq_in,
    sums, halves, keys, grads, gstage, ghalves, gfull, query, gout, gquery,
    gv_send, gv_recv, gv_far, gv_own, far_send, far_recv, tail_send, tail_recv, stat_send, stat_recv,
    pair_send, pair_recv, local_sem, act_send, act_recv, w_send, w_recv, sq_send, sq_recv,
    k_send, k_recv, g_send, g_recv, gv_sem, gv_rsem, far_sem, far_rsem, end_send, end_recv,
):
    me = lax.axis_index("seq")
    group, member = me // size, me % size
    core = me % 2
    sibling = me + 1 - 2 * core
    groups = n // size
    n_bits = int(math.log2(groups))
    bit = [(group // (1 << b)) % 2 for b in range(n_bits)]
    partner = [me + (1 - 2 * bit[b]) * (size << b) for b in range(n_bits)]
    side = member // 2
    mates = []
    for d in range(size):
        mate = member
        if d & 1:
            mate = mate + 1 - 2 * core
        if d & 2:
            mate = mate + 2 - 4 * side
        mates.append(mate)
    mate_device = [group * size + mate for mate in mates]
    near_bits = 2 if size == 2 else 1
    low = list(range(min(near_bits, n_bits)))
    high = list(range(len(low), n_bits))
    gather_order = [high + low, high + low[::-1]]
    reduce_order = [low + high, low[::-1] + high if size == 2 else high + low]
    width = wq.shape[2]
    toks = vid.shape[1]
    pending = []

    barrier = pltpu.get_barrier_semaphore()
    peers = mate_device[1:] + partner
    for peer in peers:
        pl.semaphore_signal(barrier, inc=1, device_id={"seq": peer}, device_id_type=MESH)
    pl.semaphore_wait(barrier, len(peers))

    def send(src, dst, send_sem, recv_sem, peer):
        copy = pltpu.make_async_remote_copy(
            src_ref=src, dst_ref=dst, send_sem=send_sem, recv_sem=recv_sem,
            device_id={"seq": peer}, device_id_type=MESH,
        )
        copy.start()
        pending.append(copy)
        return copy

    def part(array):
        return [array.at[:, pl.ds(pl.multiple_of(mate * width, 128), width)] for mate in mates]

    plan = [
        ([scaled] * size, st.at[member]),
        (part(w_key), wk.at[member]),
        (part(w_value), wv.at[member]),
        ([squares] * size, sq.at[member]),
        (part(w_query), wq.at[me]),
        (part(w_out), wo.at[me]),
    ]
    shared = []
    for i, (sources, dst) in enumerate(plan):
        copies = [
            send(sources[d], dst, pair_send.at[i, d], pair_recv.at[i, d], mate_device[d]) for d in range(1, size)
        ]
        local = pltpu.make_async_copy(sources[0], dst, local_sem.at[i])
        local.start()
        shared.append((copies, local))
    moving = []
    for i, (rows, buffer) in enumerate(((video, vid), (cotangent, cot))):
        dst = buffer.at[member]
        copies = [send(rows, dst, act_send.at[i, d], act_recv.at[i, d], mate_device[d]) for d in range(1, min(size, 3))]
        local = pltpu.make_async_copy(rows, dst, local_sem.at[len(plan) + i])
        local.start()
        moving.append((copies, local))

    def have(i):
        for copy in shared[i][0]:
            copy.wait_recv()
        shared[i][1].wait()

    def pass_on(i):
        if size > 2:
            moving[i][0][1].wait_recv()
            rows = (vid, cot)[i].at[mates[2]]
            moving[i][0].append(send(rows, rows, act_send.at[i, 3], act_recv.at[i, 3], mate_device[1]))

    def have_rows(i):
        copies, local = moving[i]
        copies[0].wait_recv()
        if size > 2:
            copies[2].wait_recv()
        local.wait()

    arrivals = {}

    def weights(array, buffer, p):
        for stream in range(size):
            order = gather_order[stream % 2]
            where = group
            for t in range(n_bits):
                if (p >> t) & 1:
                    where = where + (1 - 2 * bit[order[t]]) * (1 << order[t])
            block = buffer.at[size * where + stream]
            if p > 0:
                arrivals[array, stream, p].wait_recv()
            for t in range(p.bit_length(), n_bits):
                q = p + (1 << t)
                arrivals[array, stream, q] = send(
                    block, block, w_send.at[array, stream, q], w_recv.at[array, stream, q], partner[order[t]]
                )

    def reduce_gather(parts, stage, landing, full, send_sem, recv_sem, finish):
        held = parts.shape[1]
        base = [0, 0]
        sizes, bases = [], []
        offset = 0
        for step in range(n_bits):
            half = max(held // 2, 1)
            sent = []
            for i in range(2):
                b = reduce_order[i][step]
                if held > 1:
                    away = base[i] + (1 - bit[b]) * half
                    base[i] = base[i] + bit[b] * half
                else:
                    away = base[i]
                source = parts.at[i, pl.ds(away, half)]
                if stage is not None:
                    stage[i, offset : offset + half] = source[...].astype(stage.dtype)
                    source = stage.at[i, pl.ds(offset, half)]
                sent.append(
                    send(
                        source, landing.at[i, pl.ds(offset, half)],
                        send_sem.at[i, step], recv_sem.at[i, step], partner[b],
                    )
                )
            yield
            for i in range(2):
                sent[i].wait_recv()
                if held == 1:
                    sent[i].wait_send()
                    pending[:] = [copy for copy in pending if copy is not sent[i]]
                spot = pl.ds(base[i], half)
                parts[i, spot] = parts[i, spot] + landing[i, offset : offset + half].astype(F32)
            sizes.append((step, half) if held > 1 else None)
            bases.append(list(base))
            offset += half
            held = half
        for i in range(2):
            finish(i, base[i], held)
        for entry in range(n_bits - 1, -1, -1):
            if sizes[entry] is None:
                continue
            step, half = sizes[entry]
            sent = []
            for i in range(2):
                spot = full.at[i, pl.ds(bases[entry][i], half)]
                sent.append(
                    send(
                        spot, spot, send_sem.at[i, n_bits + step], recv_sem.at[i, n_bits + step],
                        partner[reduce_order[i][step]],
                    )
                )
            yield
            for i in range(2):
                sent[i].wait_recv()

    def square_sum():
        have(3)
        sq_in[0] = functools.reduce(jnp.add, [sq[m] for m in range(size)])
        for b in range(n_bits):
            copy = send(sq_in.at[b], sq.at[size + b], sq_send.at[b], sq_recv.at[b], partner[b])
            yield
            copy.wait_recv()
            sq_in[b + 1] = sq_in[b] + sq[size + b]
        inverse[...] = lax.rsqrt(sq_in[n_bits] / text_dim + epsilon)

    def drain(generator, steps=None):
        count = 0
        for _ in generator:
            count += 1
            if steps is not None and count >= steps:
                return

    pieces = sums.shape[1]
    for i in range(3):
        have(i)
    for i, w in ((0, wk), (1, wv)):
        total = functools.reduce(jnp.add, [dot(st[m], w[m], (1, 0)) for m in range(size)])
        sums[i] = total.reshape(pieces, ROWS, width)

    def finish_keys(i, base, held):
        inv = inverse[pl.ds(pl.multiple_of(base * ROWS, ROWS), held * ROWS), :][:, 0:1]
        total = sums[i, pl.ds(base, held)].reshape(held * ROWS, width)
        keys[i, pl.ds(base, held)] = (inv * total).astype(BF16).reshape(held, ROWS, width)

    text_sum = reduce_gather(sums, None, halves, keys, k_send, k_recv, finish_keys)
    norm_sum = square_sum()
    next(text_sum)
    next(norm_sum)
    have(4)
    weights(0, wq, 0)
    have(5)
    weights(1, wo, 0)
    blocks = 1 << n_bits
    near = blocks // 2
    small = [(0, wq, p) for p in range(1, near)] + [(1, wo, p) for p in range(1, near)]
    for i, event in enumerate(small):
        weights(*event)
        drain(norm_sum, 1)
        drain(text_sum, 1)
        if i == near - 2:
            pass_on(0)
    drain(norm_sum)
    drain(text_sum)
    pass_on(1)
    for p in range(near, blocks):
        weights(0, wq, p)
    have_rows(0)
    tile = 256 if width % 256 == 0 else 128

    def project(rows, w, out):
        def body(t, _):
            cols = pl.ds(pl.multiple_of(t * tile, tile), tile)
            wide = w[:, :, cols].reshape(-1, tile)
            out[:, cols] = dot(rows[...].reshape(size * toks, -1), wide, (1, 0)).astype(BF16)
            return 0

        lax.fori_loop(0, width // tile, body, 0)

    project(vid, wq, query)
    for p in range(near, blocks):
        weights(1, wo, p)
    have_rows(1)
    project(cot, wo, gout)

    scale = HEAD_DIM ** (-0.5)
    text_len = pieces * ROWS

    def attention(h, _):
        cols = pl.ds(pl.multiple_of(h * HEAD_DIM, HEAD_DIM), HEAD_DIM)
        key = keys[0, :, :, cols].reshape(text_len, HEAD_DIM)
        value = keys[1, :, :, cols].reshape(text_len, HEAD_DIM)
        q, g = query[:, cols], gout[:, cols]
        raised = jnp.exp(dot(key, q, (1, 1)) * scale)
        probs = raised / jnp.sum(raised, axis=0, keepdims=True)
        grad_probs = dot(value, g, (1, 1))
        delta = jnp.sum(grad_probs * probs, axis=0, keepdims=True)
        grad_scores = (probs * (grad_probs - delta) * scale).astype(BF16)
        gquery[:, cols] = dot(grad_scores, key, (0, 0)).astype(BF16)
        grads[0, :, :, cols] = dot(grad_scores, q, (1, 0)).reshape(pieces, ROWS, HEAD_DIM)
        grads[1, :, :, cols] = dot(probs.astype(BF16), g, (1, 0)).reshape(pieces, ROWS, HEAD_DIM)
        return 0

    lax.fori_loop(0, width // HEAD_DIM, attention, 0)

    def finish_grads(i, base, held):
        gfull[i, pl.ds(base, held)] = grads[i, pl.ds(base, held)].astype(BF16)

    grad_sum = reduce_gather(grads, gstage, ghalves, gfull, g_send, g_recv, finish_grads)
    next(grad_sum)
    span = 8 * wq.shape[1]
    tiles = n // 8
    chips = size // 2

    def back(who, t):
        wide = wq[8 * t : 8 * t + 8].reshape(span, width)
        left = gquery[pl.ds(pl.multiple_of(who * toks, toks), toks), :]
        return dot(left, wide, (1, 1))

    across, beyond = [], []

    def hand_over(t):
        cols = slice(t * span, (t + 1) * span)
        across[t].wait_recv()
        if chips > 1:
            far_send[t] = (gv_far[:, cols] + gv_recv[t, 1 - side].astype(F32)).astype(BF16)
            beyond.append(send(far_send.at[t], far_recv.at[t], far_sem.at[t], far_rsem.at[t], mate_device[2]))

    for t in range(tiles):
        cols = slice(t * span, (t + 1) * span)
        for x in range(chips):
            gv_send[t, x] = back(2 * x + 1 - core, t).astype(BF16)
        across.append(send(gv_send.at[t], gv_recv.at[t], gv_sem.at[t], gv_rsem.at[t], sibling))
        if chips > 1:
            gv_far[:, cols] = back(mates[2], t)
        drain(grad_sum, 1)
        if t > 0:
            hand_over(t - 1)
    hand_over(tiles - 1)
    for t in range(tiles):
        gv_own[:, t * span : (t + 1) * span] = back(member, t)
        drain(grad_sum, 1)
    drain(grad_sum)

    gk, gv = gfull[0].reshape(text_len, width), gfull[1].reshape(text_len, width)
    products = gk.astype(F32) * keys[0].reshape(text_len, width).astype(F32) + gv.astype(F32) * keys[1].reshape(
        text_len, width
    ).astype(F32)
    stat_send[...] = lax.dot_general(
        jnp.ones((8, width), F32), products, (((1,), (1,)), ((), ())),
        precision=lax.Precision.HIGHEST, preferred_element_type=F32,
    )
    ends = []
    for d in range(size - 1, 0, -1):
        tail_send[d - 1] = (dot(gk, wk[mates[d]], (1, 1)) + dot(gv, wv[mates[d]], (1, 1))).astype(BF16)
        ends.append(send(tail_send.at[d - 1], tail_recv.at[d - 1], end_send.at[0, d], end_recv.at[0, d], mate_device[d]))
        ends.append(send(stat_send, stat_recv.at[d - 1], end_send.at[1, d], end_recv.at[1, d], mate_device[d]))
    total = dot(gk, wk[member], (1, 1)) + dot(gv, wv[member], (1, 1))
    for t in range(tiles):
        cols = slice(t * span, (t + 1) * span)
        tile_sum = gv_own[:, cols] + gv_recv[t, side].astype(F32)
        if chips > 1:
            beyond[t].wait_recv()
            tile_sum = tile_sum + far_recv[t].astype(F32)
        grad_video[:, cols] = tile_sum.astype(BF16)
    for copy in ends:
        copy.wait_recv()
    stat = stat_send[...]
    for d in range(1, size):
        total = total + tail_recv[d - 1].astype(F32)
        stat = stat + stat_recv[d - 1]
    grad_normed[...] = total
    row_stat[...] = stat
    for copy in pending:
        copy.wait_send()


def body(n, heads_split, text_dim, video, cotangent, text_embed, text_gain, w_query, w_key, w_value, w_out):
    toks, model = video.shape
    text_len, feats = text_embed.shape
    rows = w_query.shape[0]
    heads = w_query.shape[1] // HEAD_DIM
    size = 4 if heads % 4 == 0 and n % 4 == 0 else 2
    width = w_query.shape[1] // size
    n_bits = int(math.log2(n // size))
    chips, tiles = size // 2, n // 8
    pieces = text_len // ROWS
    text_wide = text_embed.astype(F32)
    scaled = (text_wide * text_gain).astype(BF16)
    squares = jnp.broadcast_to(jnp.sum(text_wide * text_wide, axis=1, keepdims=True), (text_len, 128))
    lanes = -(-feats // 128) * 128
    if lanes > feats:
        scaled = jnp.pad(scaled, ((0, 0), (0, lanes - feats)))
        w_key, w_value = (jnp.pad(w, ((0, lanes - feats), (0, 0))) for w in (w_key, w_value))
    vmem, dma = pltpu.VMEM, pltpu.SemaphoreType.DMA
    landing = pieces + n_bits
    side = size * toks
    flops = 6 * side * model * width + 10 * side * text_len * width
    out = pl.pallas_call(
        functools.partial(kernel, n, size, text_dim),
        out_shape=[
            jax.ShapeDtypeStruct((toks, model), BF16),
            jax.ShapeDtypeStruct((text_len, lanes), F32),
            jax.ShapeDtypeStruct((8, text_len), F32),
            jax.ShapeDtypeStruct((text_len, 128), F32),
        ],
        in_specs=[pl.BlockSpec(memory_space=pl.ANY)] * 8,
        out_specs=[pl.BlockSpec(memory_space=pltpu.VMEM)] * 4,
        scratch_shapes=[
            vmem((n, rows, width), BF16),
            vmem((n, rows, width), BF16),
            vmem((size, toks, model), BF16),
            vmem((size, toks, model), BF16),
            vmem((size, lanes, width), BF16),
            vmem((size, lanes, width), BF16),
            vmem((size, text_len, lanes), BF16),
            vmem((size + n_bits, text_len, 128), F32),
            vmem((1 + n_bits, text_len, 128), F32),
            vmem((2, pieces, ROWS, width), F32),
            vmem((2, landing, ROWS, width), F32),
            vmem((2, pieces, ROWS, width), BF16),
            vmem((2, pieces, ROWS, width), F32),
            vmem((2, landing, ROWS, width), BF16),
            vmem((2, landing, ROWS, width), BF16),
            vmem((2, pieces, ROWS, width), BF16),
            vmem((side, width), BF16),
            vmem((side, width), BF16),
            vmem((side, width), BF16),
            vmem((tiles, chips, toks, model // tiles), BF16),
            vmem((tiles, chips, toks, model // tiles), BF16),
            vmem((toks, model), F32),
            vmem((toks, model), F32),
            vmem((tiles, toks, model // tiles), BF16),
            vmem((tiles, toks, model // tiles), BF16),
            vmem((size - 1, text_len, lanes), BF16),
            vmem((size - 1, text_len, lanes), BF16),
            vmem((8, text_len), F32),
            vmem((size - 1, 8, text_len), F32),
            dma((6, size)),
            dma((6, size)),
            dma((8,)),
            dma((2, 4)),
            dma((2, 4)),
            dma((2, size, n // size)),
            dma((2, size, n // size)),
            dma((n_bits,)),
            dma((n_bits,)),
            dma((2, 2 * n_bits)),
            dma((2, 2 * n_bits)),
            dma((2, 2 * n_bits)),
            dma((2, 2 * n_bits)),
            dma((tiles,)),
            dma((tiles,)),
            dma((tiles,)),
            dma((tiles,)),
            dma((2, size)),
            dma((2, size)),
        ],
        compiler_params=pltpu.CompilerParams(
            collective_id=0, has_side_effects=True, vmem_limit_bytes=60 * 1024 * 1024
        ),
        cost_estimate=pl.CostEstimate(
            flops=flops, bytes_accessed=8 * toks * model, transcendentals=side * text_len * width // HEAD_DIM
        ),
    )(scaled, squares, w_key, w_value, w_query, w_out.T, video, cotangent)
    grad_video, grad_normed, row_stat, inverse = out
    grad_normed = grad_normed[:, 0:feats]
    if heads_split > 1:
        grad_normed, row_stat = lax.psum((grad_normed, row_stat), "head")
        grad_video = lax.psum_scatter(grad_video, "head", scatter_dimension=1, tiled=True)
    inv = inverse[:, 0:1]
    grad_text = inv * (grad_normed * text_gain - text_wide * inv * (row_stat[0][:, None] / text_dim))
    return (grad_video, grad_text)


def solution(mesh):
    n, heads_split = mesh.shape["seq"], mesh.shape["head"]
    in_specs = (
        P("seq", None),
        P("seq", None),
        P(None, "seq"),
        P("seq"),
        P("seq", "head"),
        P("seq", "head"),
        P("seq", "head"),
        P("head", "seq"),
    )
    out_specs = (P("seq", "head"), P(None, "seq"))

    def whole(video, cotangent, text_embed, *rest):
        run = functools.partial(body, n, heads_split, text_embed.shape[1])
        mapped = jax.shard_map(run, mesh=mesh, in_specs=in_specs, out_specs=out_specs, check_vma=False)
        return mapped(video, cotangent, text_embed, *rest)

    return whole
```

```python
import functools
import math

import jax
import jax.numpy as jnp
from jax import lax
from jax.experimental import pallas as pl
from jax.experimental.pallas import tpu as pltpu
from jax.sharding import PartitionSpec as P

HEAD_DIM = 128
ROWS = 16
MESH = pl.DeviceIdType.MESH
epsilon = 1e-06
F32 = jnp.float32
BF16 = jnp.bfloat16


def dot(a, b, dims):
    return lax.dot_general(a, b, ((dims[0:1], dims[1:2]), ((), ())), preferred_element_type=F32)


def kernel(
    n, size, text_dim, scaled, squares, w_key, w_value, w_query, w_out, video, cotangent,
    grad_video, grad_normed, row_stat, inverse,
    wq, wo, vid, cot, wk, wv, st, sq, sq_in,
    sums, halves, keys, grads, gstage, ghalves, gfull, query, gout, gquery,
    gv_send, gv_recv, gv_far, gv_own, far_send, far_recv, tail_send, tail_recv, stat_send, stat_recv,
    pair_send, pair_recv, local_sem, act_send, act_recv, w_send, w_recv, sq_send, sq_recv,
    k_send, k_recv, g_send, g_recv, gv_sem, gv_rsem, far_sem, far_rsem, end_send, end_recv,
):
    me = lax.axis_index("seq")
    group, member = me // size, me % size
    core = me % 2
    sibling = me + 1 - 2 * core
    groups = n // size
    n_bits = int(math.log2(groups))
    bit = [(group // (1 << b)) % 2 for b in range(n_bits)]
    partner = [me + (1 - 2 * bit[b]) * (size << b) for b in range(n_bits)]
    side = member // 2
    mates = []
    for d in range(size):
        mate = member
        if d & 1:
            mate = mate + 1 - 2 * core
        if d & 2:
            mate = mate + 2 - 4 * side
        mates.append(mate)
    mate_device = [group * size + mate for mate in mates]
    near_bits = 2 if size == 2 else 1
    low = list(range(min(near_bits, n_bits)))
    high = list(range(len(low), n_bits))
    gather_order = [high + low, high + low[::-1]]
    reduce_order = [low + high, low[::-1] + high if size == 2 else high + low]
    width = wq.shape[2]
    toks = vid.shape[1]
    pending = []

    barrier = pltpu.get_barrier_semaphore()
    peers = mate_device[1:] + partner
    for peer in peers:
        pl.semaphore_signal(barrier, inc=1, device_id={"seq": peer}, device_id_type=MESH)
    pl.semaphore_wait(barrier, len(peers))

    def send(src, dst, send_sem, recv_sem, peer):
        copy = pltpu.make_async_remote_copy(
            src_ref=src, dst_ref=dst, send_sem=send_sem, recv_sem=recv_sem,
            device_id={"seq": peer}, device_id_type=MESH,
        )
        copy.start()
        pending.append(copy)
        return copy

    def part(array):
        return [array.at[:, pl.ds(pl.multiple_of(mate * width, 128), width)] for mate in mates]

    plan = [
        ([scaled] * size, st.at[member]),
        (part(w_key), wk.at[member]),
        (part(w_value), wv.at[member]),
        ([squares] * size, sq.at[member]),
        (part(w_query), wq.at[me]),
        (part(w_out), wo.at[me]),
    ]
    shared = []
    for i, (sources, dst) in enumerate(plan):
        copies = [
            send(sources[d], dst, pair_send.at[i, d], pair_recv.at[i, d], mate_device[d]) for d in range(1, size)
        ]
        local = pltpu.make_async_copy(sources[0], dst, local_sem.at[i])
        local.start()
        shared.append((copies, local))
    moving = []
    for i, (rows, buffer) in enumerate(((video, vid), (cotangent, cot))):
        dst = buffer.at[member]
        copies = [send(rows, dst, act_send.at[i, d], act_recv.at[i, d], mate_device[d]) for d in range(1, min(size, 3))]
        local = pltpu.make_async_copy(rows, dst, local_sem.at[len(plan) + i])
        local.start()
        moving.append((copies, local))

    def have(i):
        for copy in shared[i][0]:
            copy.wait_recv()
        shared[i][1].wait()

    def pass_on(i):
        if size > 2:
            moving[i][0][1].wait_recv()
            rows = (vid, cot)[i].at[mates[2]]
            moving[i][0].append(send(rows, rows, act_send.at[i, 3], act_recv.at[i, 3], mate_device[1]))

    def have_rows(i):
        copies, local = moving[i]
        copies[0].wait_recv()
        if size > 2:
            copies[2].wait_recv()
        local.wait()

    arrivals = {}

    def weights(array, buffer, p):
        for stream in range(size):
            order = gather_order[stream % 2]
            where = group
            for t in range(n_bits):
                if (p >> t) & 1:
                    where = where + (1 - 2 * bit[order[t]]) * (1 << order[t])
            block = buffer.at[size * where + stream]
            if p > 0:
                arrivals[array, stream, p].wait_recv()
            for t in range(p.bit_length(), n_bits):
                q = p + (1 << t)
                arrivals[array, stream, q] = send(
                    block, block, w_send.at[array, stream, q], w_recv.at[array, stream, q], partner[order[t]]
                )

    def reduce_gather(parts, stage, landing, full, send_sem, recv_sem, finish):
        held = parts.shape[1]
        base = [0, 0]
        sizes, bases = [], []
        offset = 0
        for step in range(n_bits):
            half = max(held // 2, 1)
            sent = []
            for i in range(2):
                b = reduce_order[i][step]
                if held > 1:
                    away = base[i] + (1 - bit[b]) * half
                    base[i] = base[i] + bit[b] * half
                else:
                    away = base[i]
                source = parts.at[i, pl.ds(away, half)]
                if stage is not None:
                    stage[i, offset : offset + half] = source[...].astype(stage.dtype)
                    source = stage.at[i, pl.ds(offset, half)]
                sent.append(
                    send(
                        source, landing.at[i, pl.ds(offset, half)],
                        send_sem.at[i, step], recv_sem.at[i, step], partner[b],
                    )
                )
            yield
            for i in range(2):
                sent[i].wait_recv()
                if held == 1:
                    sent[i].wait_send()
                    pending[:] = [copy for copy in pending if copy is not sent[i]]
                spot = pl.ds(base[i], half)
                parts[i, spot] = parts[i, spot] + landing[i, offset : offset + half].astype(F32)
            sizes.append((step, half) if held > 1 else None)
            bases.append(list(base))
            offset += half
            held = half
        for i in range(2):
            finish(i, base[i], held)
        for entry in range(n_bits - 1, -1, -1):
            if sizes[entry] is None:
                continue
            step, half = sizes[entry]
            sent = []
            for i in range(2):
                spot = full.at[i, pl.ds(bases[entry][i], half)]
                sent.append(
                    send(
                        spot, spot, send_sem.at[i, n_bits + step], recv_sem.at[i, n_bits + step],
                        partner[reduce_order[i][step]],
                    )
                )
            yield
            for i in range(2):
                sent[i].wait_recv()

    def square_sum():
        have(3)
        sq_in[0] = functools.reduce(jnp.add, [sq[m] for m in range(size)])
        for b in range(n_bits):
            copy = send(sq_in.at[b], sq.at[size + b], sq_send.at[b], sq_recv.at[b], partner[b])
            yield
            copy.wait_recv()
            sq_in[b + 1] = sq_in[b] + sq[size + b]
        inverse[...] = lax.rsqrt(sq_in[n_bits] / text_dim + epsilon)

    def drain(generator, steps=None):
        count = 0
        for _ in generator:
            count += 1
            if steps is not None and count >= steps:
                return

    pieces = sums.shape[1]
    for i in range(3):
        have(i)
    for i, w in ((0, wk), (1, wv)):
        total = functools.reduce(jnp.add, [dot(st[m], w[m], (1, 0)) for m in range(size)])
        sums[i] = total.reshape(pieces, ROWS, width)

    def finish_keys(i, base, held):
        inv = inverse[pl.ds(pl.multiple_of(base * ROWS, ROWS), held * ROWS), :][:, 0:1]
        total = sums[i, pl.ds(base, held)].reshape(held * ROWS, width)
        keys[i, pl.ds(base, held)] = (inv * total).astype(BF16).reshape(held, ROWS, width)

    text_sum = reduce_gather(sums, None, halves, keys, k_send, k_recv, finish_keys)
    norm_sum = square_sum()
    next(text_sum)
    next(norm_sum)
    have(4)
    weights(0, wq, 0)
    have(5)
    weights(1, wo, 0)
    blocks = 1 << n_bits
    near = blocks // 2
    small = [(0, wq, p) for p in range(1, near)] + [(1, wo, p) for p in range(1, near)]
    for i, event in enumerate(small):
        weights(*event)
        drain(norm_sum, 1)
        drain(text_sum, 1)
        if i == near - 2:
            pass_on(0)
    drain(norm_sum)
    drain(text_sum)
    pass_on(1)
    for p in range(near, blocks):
        weights(0, wq, p)
    have_rows(0)
    tile = 256 if width % 256 == 0 else 128

    chips = size // 2
    span_rows = 2 * toks

    def of_chip(x):
        return pl.ds(pl.multiple_of(x * span_rows, span_rows), span_rows)

    def project(rows, w, out, first, count):
        def body(t, _):
            cols = pl.ds(pl.multiple_of(t * tile, tile), tile)
            wide = w[:, :, cols].reshape(-1, tile)
            left = rows[pl.ds(first, count)].reshape(count * toks, -1)
            out[pl.ds(pl.multiple_of(first * toks, toks), count * toks), cols] = dot(left, wide, (1, 0)).astype(BF16)
            return 0

        lax.fori_loop(0, width // tile, body, 0)

    project(vid, wq, query, 0, size)
    for p in range(near, blocks):
        weights(1, wo, p)
    have_rows(1)

    scale = HEAD_DIM ** (-0.5)
    text_len = pieces * ROWS

    def attend(x, more):
        rows = of_chip(x)

        def attention(h, _):
            cols = pl.ds(pl.multiple_of(h * HEAD_DIM, HEAD_DIM), HEAD_DIM)
            key = keys[0, :, :, cols].reshape(text_len, HEAD_DIM)
            value = keys[1, :, :, cols].reshape(text_len, HEAD_DIM)
            q, g = query[rows, cols], gout[rows, cols]
            raised = jnp.exp(dot(key, q, (1, 1)) * scale)
            probs = raised * (1.0 / jnp.sum(raised, axis=0, keepdims=True))
            grad_probs = dot(value, g, (1, 1))
            delta = jnp.sum(grad_probs * probs, axis=0, keepdims=True)
            grad_scores = (probs * (grad_probs - delta) * scale).astype(BF16)
            gquery[rows, cols] = dot(grad_scores, key, (0, 0)).astype(BF16)
            gk = dot(grad_scores, q, (1, 0)).reshape(pieces, ROWS, HEAD_DIM)
            gv = dot(probs.astype(BF16), g, (1, 0)).reshape(pieces, ROWS, HEAD_DIM)
            grads[0, :, :, cols] = grads[0, :, :, cols] + gk if more else gk
            grads[1, :, :, cols] = grads[1, :, :, cols] + gv if more else gv
            return 0

        lax.fori_loop(0, width // HEAD_DIM, attention, 0)

    def finish_grads(i, base, held):
        gfull[i, pl.ds(base, held)] = grads[i, pl.ds(base, held)].astype(BF16)

    span = 8 * wq.shape[1]
    tiles = n // 8

    def back(who, t):
        wide = wq[8 * t : 8 * t + 8].reshape(span, width)
        left = gquery[pl.ds(pl.multiple_of(who * toks, toks), toks), :]
        return dot(left, wide, (1, 1))

    def columns(t):
        return slice(t * span, (t + 1) * span)

    across, beyond = [], []
    if chips > 1:
        project(cot, wo, gout, 2 - 2 * side, 2)
        attend(1 - side, False)

        def hand_over(t):
            across[t].wait_recv()
            far_send[t] = (gv_far[:, columns(t)] + gv_recv[t, 1].astype(F32)).astype(BF16)
            beyond.append(send(far_send.at[t], far_recv.at[t], far_sem.at[t], far_rsem.at[t], mate_device[2]))

        for t in range(tiles):
            gv_send[t, 1] = back(mates[3], t).astype(BF16)
            across.append(send(gv_send.at[t, 1], gv_recv.at[t, 1], gv_sem.at[t, 1], gv_rsem.at[t, 1], sibling))
            gv_far[:, columns(t)] = back(mates[2], t)
            if t > 0:
                hand_over(t - 1)
        hand_over(tiles - 1)
    project(cot, wo, gout, 2 * side, 2)
    attend(side, chips > 1)
    grad_sum = reduce_gather(grads, gstage, ghalves, gfull, g_send, g_recv, finish_grads)
    next(grad_sum)
    near_copies = []
    for t in range(tiles):
        gv_send[t, 0] = back(mates[1], t).astype(BF16)
        near_copies.append(send(gv_send.at[t, 0], gv_recv.at[t, 0], gv_sem.at[t, 0], gv_rsem.at[t, 0], sibling))
        drain(grad_sum, 1)
    for t in range(tiles):
        gv_own[:, columns(t)] = back(member, t)
        drain(grad_sum, 1)
    drain(grad_sum)

    gk, gv = gfull[0].reshape(text_len, width), gfull[1].reshape(text_len, width)
    products = gk.astype(F32) * keys[0].reshape(text_len, width).astype(F32) + gv.astype(F32) * keys[1].reshape(
        text_len, width
    ).astype(F32)
    stat_send[...] = lax.dot_general(
        jnp.ones((8, width), F32), products, (((1,), (1,)), ((), ())),
        precision=lax.Precision.HIGHEST, preferred_element_type=F32,
    )
    ends = []
    for d in range(size - 1, 0, -1):
        tail_send[d - 1] = (dot(gk, wk[mates[d]], (1, 1)) + dot(gv, wv[mates[d]], (1, 1))).astype(BF16)
        ends.append(send(tail_send.at[d - 1], tail_recv.at[d - 1], end_send.at[0, d], end_recv.at[0, d], mate_device[d]))
        ends.append(send(stat_send, stat_recv.at[d - 1], end_send.at[1, d], end_recv.at[1, d], mate_device[d]))
    total = dot(gk, wk[member], (1, 1)) + dot(gv, wv[member], (1, 1))
    for t in range(tiles):
        cols = columns(t)
        near_copies[t].wait_recv()
        tile_sum = gv_own[:, cols] + gv_recv[t, 0].astype(F32)
        if chips > 1:
            beyond[t].wait_recv()
            tile_sum = tile_sum + far_recv[t].astype(F32)
        grad_video[:, cols] = tile_sum.astype(BF16)
    for copy in ends:
        copy.wait_recv()
    stat = stat_send[...]
    for d in range(1, size):
        total = total + tail_recv[d - 1].astype(F32)
        stat = stat + stat_recv[d - 1]
    grad_normed[...] = total
    row_stat[...] = stat
    for copy in pending:
        copy.wait_send()


def body(n, heads_split, text_dim, video, cotangent, text_embed, text_gain, w_query, w_key, w_value, w_out):
    toks, model = video.shape
    text_len, feats = text_embed.shape
    rows = w_query.shape[0]
    heads = w_query.shape[1] // HEAD_DIM
    size = 4 if heads % 4 == 0 and n % 4 == 0 else 2
    width = w_query.shape[1] // size
    n_bits = int(math.log2(n // size))
    chips, tiles = size // 2, n // 8
    pieces = text_len // ROWS
    text_wide = text_embed.astype(F32)
    scaled = (text_wide * text_gain).astype(BF16)
    squares = jnp.broadcast_to(jnp.sum(text_wide * text_wide, axis=1, keepdims=True), (text_len, 128))
    lanes = -(-feats // 128) * 128
    if lanes > feats:
        scaled = jnp.pad(scaled, ((0, 0), (0, lanes - feats)))
        w_key, w_value = (jnp.pad(w, ((0, lanes - feats), (0, 0))) for w in (w_key, w_value))
    vmem, dma = pltpu.VMEM, pltpu.SemaphoreType.DMA
    landing = pieces + n_bits
    side = size * toks
    flops = 6 * side * model * width + 10 * side * text_len * width
    out = pl.pallas_call(
        functools.partial(kernel, n, size, text_dim),
        out_shape=[
            jax.ShapeDtypeStruct((toks, model), BF16),
            jax.ShapeDtypeStruct((text_len, lanes), F32),
            jax.ShapeDtypeStruct((8, text_len), F32),
            jax.ShapeDtypeStruct((text_len, 128), F32),
        ],
        in_specs=[pl.BlockSpec(memory_space=pl.ANY)] * 8,
        out_specs=[pl.BlockSpec(memory_space=pltpu.VMEM)] * 4,
        scratch_shapes=[
            vmem((n, rows, width), BF16),
            vmem((n, rows, width), BF16),
            vmem((size, toks, model), BF16),
            vmem((size, toks, model), BF16),
            vmem((size, lanes, width), BF16),
            vmem((size, lanes, width), BF16),
            vmem((size, text_len, lanes), BF16),
            vmem((size + n_bits, text_len, 128), F32),
            vmem((1 + n_bits, text_len, 128), F32),
            vmem((2, pieces, ROWS, width), F32),
            vmem((2, landing, ROWS, width), F32),
            vmem((2, pieces, ROWS, width), BF16),
            vmem((2, pieces, ROWS, width), F32),
            vmem((2, landing, ROWS, width), BF16),
            vmem((2, landing, ROWS, width), BF16),
            vmem((2, pieces, ROWS, width), BF16),
            vmem((side, width), BF16),
            vmem((side, width), BF16),
            vmem((side, width), BF16),
            vmem((tiles, chips, toks, model // tiles), BF16),
            vmem((tiles, chips, toks, model // tiles), BF16),
            vmem((toks, model), F32),
            vmem((toks, model), F32),
            vmem((tiles, toks, model // tiles), BF16),
            vmem((tiles, toks, model // tiles), BF16),
            vmem((size - 1, text_len, lanes), BF16),
            vmem((size - 1, text_len, lanes), BF16),
            vmem((8, text_len), F32),
            vmem((size - 1, 8, text_len), F32),
            dma((6, size)),
            dma((6, size)),
            dma((8,)),
            dma((2, 4)),
            dma((2, 4)),
            dma((2, size, n // size)),
            dma((2, size, n // size)),
            dma((n_bits,)),
            dma((n_bits,)),
            dma((2, 2 * n_bits)),
            dma((2, 2 * n_bits)),
            dma((2, 2 * n_bits)),
            dma((2, 2 * n_bits)),
            dma((tiles, 2)),
            dma((tiles, 2)),
            dma((tiles,)),
            dma((tiles,)),
            dma((2, size)),
            dma((2, size)),
        ],
        compiler_params=pltpu.CompilerParams(
            collective_id=0, has_side_effects=True, vmem_limit_bytes=60 * 1024 * 1024
        ),
        cost_estimate=pl.CostEstimate(
            flops=flops, bytes_accessed=8 * toks * model, transcendentals=side * text_len * width // HEAD_DIM
        ),
    )(scaled, squares, w_key, w_value, w_query, w_out.T, video, cotangent)
    grad_video, grad_normed, row_stat, inverse = out
    grad_normed = grad_normed[:, 0:feats]
    if heads_split > 1:
        grad_normed, row_stat = lax.psum((grad_normed, row_stat), "head")
        grad_video = lax.psum_scatter(grad_video, "head", scatter_dimension=1, tiled=True)
    inv = inverse[:, 0:1]
    grad_text = inv * (grad_normed * text_gain - text_wide * inv * (row_stat[0][:, None] / text_dim))
    return (grad_video, grad_text)


def solution(mesh):
    n, heads_split = mesh.shape["seq"], mesh.shape["head"]
    in_specs = (
        P("seq", None),
        P("seq", None),
        P(None, "seq"),
        P("seq"),
        P("seq", "head"),
        P("seq", "head"),
        P("seq", "head"),
        P("head", "seq"),
    )
    out_specs = (P("seq", "head"), P(None, "seq"))

    def whole(video, cotangent, text_embed, *rest):
        run = functools.partial(body, n, heads_split, text_embed.shape[1])
        mapped = jax.shard_map(run, mesh=mesh, in_specs=in_specs, out_specs=out_specs, check_vma=False)
        return mapped(video, cotangent, text_embed, *rest)

    return whole
```

```python
import functools
import math

import jax
import jax.numpy as jnp
from jax import lax
from jax.experimental import pallas as pl
from jax.experimental.pallas import tpu as pltpu
from jax.sharding import PartitionSpec as P

HEAD_DIM = 128
ROWS = 16
MESH = pl.DeviceIdType.MESH
epsilon = 1e-06
F32 = jnp.float32
BF16 = jnp.bfloat16


def dot(a, b, dims):
    return lax.dot_general(a, b, ((dims[0:1], dims[1:2]), ((), ())), preferred_element_type=F32)


def kernel(
    n, size, text_dim, scaled, squares, w_key, w_value, w_query, w_out, video, cotangent,
    grad_video, grad_normed, row_stat, inverse,
    wq, wo, vid, cot, wk, wv, st, sq, sq_in,
    sums, halves, keys, grads, gstage, ghalves, gfull, query, gout, gquery, wqt,
    gv_send, gv_recv, gv_mine, far_send, far_recv, tail_send, tail_recv, stat_send, stat_recv,
    pair_send, pair_recv, local_sem, act_send, act_recv, w_send, w_recv, sq_send, sq_recv,
    k_send, k_recv, g_send, g_recv, gv_sem, gv_rsem, far_sem, far_rsem, end_send, end_recv,
):
    me = lax.axis_index("seq")
    group, member = me // size, me % size
    core = me % 2
    sibling = me + 1 - 2 * core
    groups = n // size
    n_bits = int(math.log2(groups))
    bit = [(group // (1 << b)) % 2 for b in range(n_bits)]
    partner = [me + (1 - 2 * bit[b]) * (size << b) for b in range(n_bits)]
    side = member // 2
    mates = []
    for d in range(size):
        mate = member
        if d & 1:
            mate = mate + 1 - 2 * core
        if d & 2:
            mate = mate + 2 - 4 * side
        mates.append(mate)
    mate_device = [group * size + mate for mate in mates]
    near_bits = 2 if size == 2 else 1
    low = list(range(min(near_bits, n_bits)))
    high = list(range(len(low), n_bits))
    gather_order = [high + low, high + low[::-1]]
    reduce_order = [low + high, low[::-1] + high if size == 2 else high + low]
    width = wq.shape[2]
    toks = vid.shape[1]
    pending = []

    barrier = pltpu.get_barrier_semaphore()
    peers = mate_device[1:] + partner
    for peer in peers:
        pl.semaphore_signal(barrier, inc=1, device_id={"seq": peer}, device_id_type=MESH)
    pl.semaphore_wait(barrier, len(peers))

    def send(src, dst, send_sem, recv_sem, peer):
        copy = pltpu.make_async_remote_copy(
            src_ref=src, dst_ref=dst, send_sem=send_sem, recv_sem=recv_sem,
            device_id={"seq": peer}, device_id_type=MESH,
        )
        copy.start()
        pending.append(copy)
        return copy

    def part(array):
        return [array.at[:, pl.ds(pl.multiple_of(mate * width, 128), width)] for mate in mates]

    plan = [
        ([scaled] * size, st.at[member]),
        (part(w_key), wk.at[member]),
        (part(w_value), wv.at[member]),
        ([squares] * size, sq.at[member]),
        (part(w_query), wq.at[me]),
        (part(w_out), wo.at[me]),
    ]
    shared = []
    for i, (sources, dst) in enumerate(plan):
        copies = [
            send(sources[d], dst, pair_send.at[i, d], pair_recv.at[i, d], mate_device[d]) for d in range(1, size)
        ]
        local = pltpu.make_async_copy(sources[0], dst, local_sem.at[i])
        local.start()
        shared.append((copies, local))
    chips = size // 2
    cuts = 4
    piece = toks // cuts
    slots = [(mate % 2) * chips + mate // 2 for mate in mates]
    moving = [[], []]
    own_rows = []
    for i, (rows, buffer) in enumerate(((video, vid), (cotangent, cot))):
        local = pltpu.make_async_copy(rows, buffer.at[slots[0]], local_sem.at[len(plan) + i])
        local.start()
        own_rows.append(local)

    def move(i, c):
        rows, buffer = ((video, vid), (cotangent, cot))[i]
        cut = pl.ds(c * piece, piece)
        dst = buffer.at[slots[0], cut]
        moving[i].append(
            [send(rows.at[cut], dst, act_send.at[i, c, d], act_recv.at[i, c, d], mate_device[d]) for d in range(min(size, 3) - 1, 0, -1)]
        )

    def have(i):
        for copy in shared[i][0]:
            copy.wait_recv()
        shared[i][1].wait()

    def pass_on(i):
        if size > 2:
            for c in range(cuts):
                copies = moving[i][c]
                copies[0].wait_recv()
                rows = (vid, cot)[i].at[slots[2], pl.ds(c * piece, piece)]
                copies.append(send(rows, rows, act_send.at[i, c, 3], act_recv.at[i, c, 3], mate_device[1]))

    def have_rows(i):
        for copies in moving[i]:
            for copy in copies[1:] if size > 2 else copies:
                copy.wait_recv()
        own_rows[i].wait()

    arrivals = {}

    def weights(array, buffer, p):
        for stream in range(size):
            order = gather_order[stream % 2]
            where = group
            for t in range(n_bits):
                if (p >> t) & 1:
                    where = where + (1 - 2 * bit[order[t]]) * (1 << order[t])
            block = buffer.at[size * where + stream]
            if p > 0:
                arrivals[array, stream, p].wait_recv()
            for t in range(p.bit_length(), n_bits):
                q = p + (1 << t)
                arrivals[array, stream, q] = send(
                    block, block, w_send.at[array, stream, q], w_recv.at[array, stream, q], partner[order[t]]
                )

    def reduce_gather(parts, stage, landing, full, send_sem, recv_sem, finish):
        held = parts.shape[1]
        base = [0, 0]
        sizes, bases = [], []
        offset = 0
        for step in range(n_bits):
            half = max(held // 2, 1)
            sent = []
            for i in range(2):
                b = reduce_order[i][step]
                if held > 1:
                    away = base[i] + (1 - bit[b]) * half
                    base[i] = base[i] + bit[b] * half
                else:
                    away = base[i]
                source = parts.at[i, pl.ds(away, half)]
                if stage is not None:
                    stage[i, offset : offset + half] = source[...].astype(stage.dtype)
                    source = stage.at[i, pl.ds(offset, half)]
                sent.append(
                    send(
                        source, landing.at[i, pl.ds(offset, half)],
                        send_sem.at[i, step], recv_sem.at[i, step], partner[b],
                    )
                )
            yield
            for i in range(2):
                sent[i].wait_recv()
                if held == 1:
                    sent[i].wait_send()
                    pending[:] = [copy for copy in pending if copy is not sent[i]]
                spot = pl.ds(base[i], half)
                parts[i, spot] = parts[i, spot] + landing[i, offset : offset + half].astype(F32)
            sizes.append((step, half) if held > 1 else None)
            bases.append(list(base))
            offset += half
            held = half
        for i in range(2):
            finish(i, base[i], held)
        for entry in range(n_bits - 1, -1, -1):
            if sizes[entry] is None:
                continue
            step, half = sizes[entry]
            sent = []
            for i in range(2):
                spot = full.at[i, pl.ds(bases[entry][i], half)]
                sent.append(
                    send(
                        spot, spot, send_sem.at[i, n_bits + step], recv_sem.at[i, n_bits + step],
                        partner[reduce_order[i][step]],
                    )
                )
            yield
            for i in range(2):
                sent[i].wait_recv()

    def square_sum():
        have(3)
        sq_in[0] = functools.reduce(jnp.add, [sq[m] for m in range(size)])
        for b in range(n_bits):
            copy = send(sq_in.at[b], sq.at[size + b], sq_send.at[b], sq_recv.at[b], partner[b])
            yield
            copy.wait_recv()
            sq_in[b + 1] = sq_in[b] + sq[size + b]
        inverse[...] = lax.rsqrt(sq_in[n_bits] / text_dim + epsilon)

    def drain(generator, steps=None):
        count = 0
        for _ in generator:
            count += 1
            if steps is not None and count >= steps:
                return

    pieces = sums.shape[1]
    def finish_keys(i, base, held):
        inv = inverse[pl.ds(pl.multiple_of(base * ROWS, ROWS), held * ROWS), :][:, 0:1]
        total = sums[i, pl.ds(base, held)].reshape(held * ROWS, width)
        keys[i, pl.ds(base, held)] = (inv * total).astype(BF16).reshape(held, ROWS, width)

    text_sum = reduce_gather(sums, None, halves, keys, k_send, k_recv, finish_keys)
    norm_sum = square_sum()
    have(4)
    weights(0, wq, 0)
    for i in range(3):
        have(i)
    for i, w in ((0, wk), (1, wv)):
        total = functools.reduce(jnp.add, [dot(st[m], w[m], (1, 0)) for m in range(size)])
        sums[i] = total.reshape(pieces, ROWS, width)

    next(text_sum)
    next(norm_sum)
    have(5)
    weights(1, wo, 0)
    for c in range(cuts):
        move(0, c)
    blocks = 1 << n_bits
    near = blocks // 2
    for p in range(1, near):
        weights(0, wq, p)
        drain(norm_sum, 1)
        if p >= 2:
            drain(text_sum, 1)
        weights(1, wo, p)
        if p == 1:
            for c in range(cuts):
                move(1, c)
        else:
            drain(norm_sum, 1)
            drain(text_sum, 1)
        if p == 2:
            pass_on(0)
    pass_on(1)
    drain(norm_sum)
    for p in range(near, blocks):
        weights(0, wq, p)
    have_rows(0)
    tile = 256 if width % 256 == 0 else 128

    def project(rows, w, out):
        def body(t, _):
            cols = pl.ds(pl.multiple_of(t * tile, tile), tile)
            wide = w[:, :, cols].reshape(-1, tile)
            out[:, cols] = dot(rows[...].reshape(size * toks, -1), wide, (1, 0)).astype(BF16)
            return 0

        lax.fori_loop(0, width // tile, body, 0)

    project(vid, wq, query)
    span = 8 * wq.shape[1]
    tiles = n // 8
    for t in range(tiles):
        wqt[:, t * span : (t + 1) * span] = wq[8 * t : 8 * t + 8].reshape(span, width).T
    drain(text_sum)
    for p in range(near, blocks):
        weights(1, wo, p)
    have_rows(1)
    project(cot, wo, gout)

    scale = HEAD_DIM ** (-0.5)
    text_len = pieces * ROWS

    def attention(h, _):
        cols = pl.ds(pl.multiple_of(h * HEAD_DIM, HEAD_DIM), HEAD_DIM)
        key = keys[0, :, :, cols].reshape(text_len, HEAD_DIM)
        value = keys[1, :, :, cols].reshape(text_len, HEAD_DIM)
        q, g = query[:, cols], gout[:, cols]
        raised = jnp.exp(dot(key, q, (1, 1)) * scale)
        probs = raised * (1.0 / jnp.sum(raised, axis=0, keepdims=True))
        grad_probs = dot(value, g, (1, 1))
        delta = jnp.sum(grad_probs * probs, axis=0, keepdims=True)
        grad_scores = (probs * (grad_probs - delta) * scale).astype(BF16)
        gquery[:, cols] = dot(grad_scores, key, (0, 0)).astype(BF16)
        grads[0, :, :, cols] = dot(grad_scores, q, (1, 0)).reshape(pieces, ROWS, HEAD_DIM)
        grads[1, :, :, cols] = dot(probs.astype(BF16), g, (1, 0)).reshape(pieces, ROWS, HEAD_DIM)
        return 0

    lax.fori_loop(0, width // HEAD_DIM, attention, 0)

    def finish_grads(i, base, held):
        gfull[i, pl.ds(base, held)] = grads[i, pl.ds(base, held)].astype(BF16)

    grad_sum = reduce_gather(grads, gstage, ghalves, gfull, g_send, g_recv, finish_grads)
    next(grad_sum)
    half_rows = chips * toks

    def back(who, t):
        left = gquery[pl.ds(pl.multiple_of(who * half_rows, half_rows), half_rows), :]
        return dot(left, wqt[:, t * span : (t + 1) * span], (1, 0)).reshape(chips, toks, span)

    across, beyond = [], []

    def hand_over(t):
        across[t].wait_recv()
        if chips > 1:
            far_send[t] = (gv_mine[t, 1 - side] + gv_recv[t, 1 - side].astype(F32)).astype(BF16)
            beyond.append(send(far_send.at[t], far_recv.at[t], far_sem.at[t], far_rsem.at[t], mate_device[2]))

    for t in range(tiles):
        gv_send[t] = back(1 - core, t).astype(BF16)
        across.append(send(gv_send.at[t], gv_recv.at[t], gv_sem.at[t], gv_rsem.at[t], sibling))
        gv_mine[t] = back(core, t)
        drain(grad_sum, 1)
        if t > 0:
            hand_over(t - 1)
    hand_over(tiles - 1)
    drain(grad_sum)

    gk, gv = gfull[0].reshape(text_len, width), gfull[1].reshape(text_len, width)
    products = gk.astype(F32) * keys[0].reshape(text_len, width).astype(F32) + gv.astype(F32) * keys[1].reshape(
        text_len, width
    ).astype(F32)
    stat_send[...] = lax.dot_general(
        jnp.ones((8, width), F32), products, (((1,), (1,)), ((), ())),
        precision=lax.Precision.HIGHEST, preferred_element_type=F32,
    )
    ends = []
    for d in range(size - 1, 0, -1):
        tail_send[d - 1] = (dot(gk, wk[mates[d]], (1, 1)) + dot(gv, wv[mates[d]], (1, 1))).astype(BF16)
        ends.append(send(tail_send.at[d - 1], tail_recv.at[d - 1], end_send.at[0, d], end_recv.at[0, d], mate_device[d]))
        ends.append(send(stat_send, stat_recv.at[d - 1], end_send.at[1, d], end_recv.at[1, d], mate_device[d]))
    total = dot(gk, wk[member], (1, 1)) + dot(gv, wv[member], (1, 1))
    for t in range(tiles):
        cols = slice(t * span, (t + 1) * span)
        tile_sum = gv_mine[t, side] + gv_recv[t, side].astype(F32)
        if chips > 1:
            beyond[t].wait_recv()
            tile_sum = tile_sum + far_recv[t].astype(F32)
        grad_video[:, cols] = tile_sum.astype(BF16)
    for copy in ends:
        copy.wait_recv()
    stat = stat_send[...]
    for d in range(1, size):
        total = total + tail_recv[d - 1].astype(F32)
        stat = stat + stat_recv[d - 1]
    grad_normed[...] = total
    row_stat[...] = stat
    for copy in pending:
        copy.wait_send()


def body(n, heads_split, text_dim, video, cotangent, text_embed, text_gain, w_query, w_key, w_value, w_out):
    toks, model = video.shape
    text_len, feats = text_embed.shape
    rows = w_query.shape[0]
    heads = w_query.shape[1] // HEAD_DIM
    size = 4 if heads % 4 == 0 and n % 4 == 0 else 2
    width = w_query.shape[1] // size
    n_bits = int(math.log2(n // size))
    chips, tiles = size // 2, n // 8
    pieces = text_len // ROWS
    text_wide = text_embed.astype(F32)
    scaled = (text_wide * text_gain).astype(BF16)
    squares = jnp.broadcast_to(jnp.sum(text_wide * text_wide, axis=1, keepdims=True), (text_len, 128))
    lanes = -(-feats // 128) * 128
    if lanes > feats:
        scaled = jnp.pad(scaled, ((0, 0), (0, lanes - feats)))
        w_key, w_value = (jnp.pad(w, ((0, lanes - feats), (0, 0))) for w in (w_key, w_value))
    vmem, dma = pltpu.VMEM, pltpu.SemaphoreType.DMA
    landing = pieces + n_bits
    side = size * toks
    flops = 6 * side * model * width + 10 * side * text_len * width
    out = pl.pallas_call(
        functools.partial(kernel, n, size, text_dim),
        out_shape=[
            jax.ShapeDtypeStruct((toks, model), BF16),
            jax.ShapeDtypeStruct((text_len, lanes), F32),
            jax.ShapeDtypeStruct((8, text_len), F32),
            jax.ShapeDtypeStruct((text_len, 128), F32),
        ],
        in_specs=[pl.BlockSpec(memory_space=pl.ANY)] * 8,
        out_specs=[pl.BlockSpec(memory_space=pltpu.VMEM)] * 4,
        scratch_shapes=[
            vmem((n, rows, width), BF16),
            vmem((n, rows, width), BF16),
            vmem((size, toks, model), BF16),
            vmem((size, toks, model), BF16),
            vmem((size, lanes, width), BF16),
            vmem((size, lanes, width), BF16),
            vmem((size, text_len, lanes), BF16),
            vmem((size + n_bits, text_len, 128), F32),
            vmem((1 + n_bits, text_len, 128), F32),
            vmem((2, pieces, ROWS, width), F32),
            vmem((2, landing, ROWS, width), F32),
            vmem((2, pieces, ROWS, width), BF16),
            vmem((2, pieces, ROWS, width), F32),
            vmem((2, landing, ROWS, width), BF16),
            vmem((2, landing, ROWS, width), BF16),
            vmem((2, pieces, ROWS, width), BF16),
            vmem((side, width), BF16),
            vmem((side, width), BF16),
            vmem((side, width), BF16),
            vmem((width, model), BF16),
            vmem((tiles, chips, toks, model // tiles), BF16),
            vmem((tiles, chips, toks, model // tiles), BF16),
            vmem((tiles, chips, toks, model // tiles), F32),
            vmem((tiles, toks, model // tiles), BF16),
            vmem((tiles, toks, model // tiles), BF16),
            vmem((size - 1, text_len, lanes), BF16),
            vmem((size - 1, text_len, lanes), BF16),
            vmem((8, text_len), F32),
            vmem((size - 1, 8, text_len), F32),
            dma((6, size)),
            dma((6, size)),
            dma((8,)),
            dma((2, 4, 4)),
            dma((2, 4, 4)),
            dma((2, size, n // size)),
            dma((2, size, n // size)),
            dma((n_bits,)),
            dma((n_bits,)),
            dma((2, 2 * n_bits)),
            dma((2, 2 * n_bits)),
            dma((2, 2 * n_bits)),
            dma((2, 2 * n_bits)),
            dma((tiles,)),
            dma((tiles,)),
            dma((tiles,)),
            dma((tiles,)),
            dma((2, size)),
            dma((2, size)),
        ],
        compiler_params=pltpu.CompilerParams(
            collective_id=0, has_side_effects=True, vmem_limit_bytes=63 * 1024 * 1024
        ),
        cost_estimate=pl.CostEstimate(
            flops=flops, bytes_accessed=8 * toks * model, transcendentals=side * text_len * width // HEAD_DIM
        ),
    )(scaled, squares, w_key, w_value, w_query, w_out.T, video, cotangent)
    grad_video, grad_normed, row_stat, inverse = out
    grad_normed = grad_normed[:, 0:feats]
    if heads_split > 1:
        grad_normed, row_stat = lax.psum((grad_normed, row_stat), "head")
        grad_video = lax.psum_scatter(grad_video, "head", scatter_dimension=1, tiled=True)
    inv = inverse[:, 0:1]
    grad_text = inv * (grad_normed * text_gain - text_wide * inv * (row_stat[0][:, None] / text_dim))
    return (grad_video, grad_text)


def solution(mesh):
    n, heads_split = mesh.shape["seq"], mesh.shape["head"]
    in_specs = (
        P("seq", None),
        P("seq", None),
        P(None, "seq"),
        P("seq"),
        P("seq", "head"),
        P("seq", "head"),
        P("seq", "head"),
        P("head", "seq"),
    )
    out_specs = (P("seq", "head"), P(None, "seq"))

    def whole(video, cotangent, text_embed, *rest):
        run = functools.partial(body, n, heads_split, text_embed.shape[1])
        mapped = jax.shard_map(run, mesh=mesh, in_specs=in_specs, out_specs=out_specs, check_vma=False)
        return mapped(video, cotangent, text_embed, *rest)

    return whole
```

```python
import functools
import math

import jax
import jax.numpy as jnp
from jax import lax
from jax.experimental import pallas as pl
from jax.experimental.pallas import tpu as pltpu
from jax.sharding import PartitionSpec as P

HEAD_DIM = 128
ROWS = 16
MESH = pl.DeviceIdType.MESH
epsilon = 1e-06
F32 = jnp.float32
BF16 = jnp.bfloat16


def dot(a, b, dims):
    return lax.dot_general(a, b, ((dims[0:1], dims[1:2]), ((), ())), preferred_element_type=F32)


def kernel(
    n, size, text_dim, scaled, squares, w_key, w_value, w_query, w_out, video, cotangent,
    grad_video, grad_normed, row_stat, inverse,
    wq, wo, vid, cot, wk, wv, st, sq, sq_in,
    sums, halves, keys, grads, gstage, ghalves, gfull, query, gout, gquery, wqt,
    gv_send, gv_recv, gv_mine, far_send, far_recv, tail_send, tail_recv, stat_send, stat_recv,
    pair_send, pair_recv, local_sem, act_send, act_recv, w_send, w_recv, n_send, n_recv, sq_send, sq_recv,
    k_send, k_recv, g_send, g_recv, gv_sem, gv_rsem, far_sem, far_rsem, end_send, end_recv,
):
    me = lax.axis_index("seq")
    group, member = me // size, me % size
    core = me % 2
    sibling = me + 1 - 2 * core
    groups = n // size
    n_bits = int(math.log2(groups))
    bit = [(group // (1 << b)) % 2 for b in range(n_bits)]
    partner = [me + (1 - 2 * bit[b]) * (size << b) for b in range(n_bits)]
    side = member // 2
    mates = []
    for d in range(size):
        mate = member
        if d & 1:
            mate = mate + 1 - 2 * core
        if d & 2:
            mate = mate + 2 - 4 * side
        mates.append(mate)
    mate_device = [group * size + mate for mate in mates]
    near_bits = 2 if size == 2 else 1
    low = list(range(min(near_bits, n_bits)))
    high = list(range(len(low), n_bits))
    reduce_order = [low + high, low[::-1] + high if size == 2 else high + low]
    width = wq.shape[2]
    toks = vid.shape[1]
    pending = []

    line = 1 << len(high)
    near_count = 1 << len(low)
    place = group // near_count
    line_peer = (me + size * near_count, me - size * near_count)
    barrier = pltpu.get_barrier_semaphore()
    peers = mate_device[1:] + partner
    for peer in peers:
        pl.semaphore_signal(barrier, inc=1, device_id={"seq": peer}, device_id_type=MESH)
    for more, peer in ((place < line - 1, line_peer[0]), (place > 0, line_peer[1])):

        @pl.when(more)
        def _():
            pl.semaphore_signal(barrier, inc=1, device_id={"seq": peer}, device_id_type=MESH)

    ends_count = (place + line - 1) // line + (2 * line - 2 - place) // line
    pl.semaphore_wait(barrier, len(peers) + ends_count)

    def send(src, dst, send_sem, recv_sem, peer):
        copy = pltpu.make_async_remote_copy(
            src_ref=src, dst_ref=dst, send_sem=send_sem, recv_sem=recv_sem,
            device_id={"seq": peer}, device_id_type=MESH,
        )
        copy.start()
        pending.append(copy)
        return copy

    def part(array):
        return [array.at[:, pl.ds(pl.multiple_of(mate * width, 128), width)] for mate in mates]

    plan = [
        ([scaled] * size, st.at[member]),
        (part(w_key), wk.at[member]),
        (part(w_value), wv.at[member]),
        ([squares] * size, sq.at[member]),
        (part(w_query), wq.at[me]),
        (part(w_out), wo.at[me]),
    ]
    shared = []
    for i, (sources, dst) in enumerate(plan):
        copies = [
            send(sources[d], dst, pair_send.at[i, d], pair_recv.at[i, d], mate_device[d]) for d in range(1, size)
        ]
        local = pltpu.make_async_copy(sources[0], dst, local_sem.at[i])
        local.start()
        shared.append((copies, local))
    chips = size // 2
    cuts = 4
    piece = toks // cuts
    slots = [(mate % 2) * chips + mate // 2 for mate in mates]
    moving = [[], []]
    own_rows = []
    for i, (rows, buffer) in enumerate(((video, vid), (cotangent, cot))):
        local = pltpu.make_async_copy(rows, buffer.at[slots[0]], local_sem.at[len(plan) + i])
        local.start()
        own_rows.append(local)

    def move(i, c):
        rows, buffer = ((video, vid), (cotangent, cot))[i]
        cut = pl.ds(c * piece, piece)
        dst = buffer.at[slots[0], cut]
        moving[i].append(
            [send(rows.at[cut], dst, act_send.at[i, c, d], act_recv.at[i, c, d], mate_device[d]) for d in range(min(size, 3) - 1, 0, -1)]
        )

    def have(i):
        for copy in shared[i][0]:
            copy.wait_recv()
        shared[i][1].wait()

    def pass_on(i):
        if size > 2:
            for c in range(cuts):
                copies = moving[i][c]
                copies[0].wait_recv()
                rows = (vid, cot)[i].at[slots[2], pl.ds(c * piece, piece)]
                copies.append(send(rows, rows, act_send.at[i, c, 3], act_recv.at[i, c, 3], mate_device[1]))

    def have_rows(i):
        for copies in moving[i]:
            for copy in copies[1:] if size > 2 else copies:
                copy.wait_recv()
        own_rows[i].wait()

    late = []

    def when(condition, run):
        if condition is None:
            run()
        else:
            pl.when(condition)(run)

    def exists(way, k):
        if k == 0:
            return None
        return place >= k if way == 0 else place < line - k

    def block(buffer, stream, way, k, pattern=0):
        where = group + (k if way else -k) * near_count
        order = low if stream % 2 == 0 else low[::-1]
        for t in range(len(low)):
            if (pattern >> t) & 1:
                where = where + (1 - 2 * bit[order[t]]) * (1 << order[t])
        return buffer.at[size * where + stream]

    def line_copy(array, buffer, stream, way, k, at):
        spot = block(buffer, stream, way, at)
        i = ((array * size + stream) * 2 + way) * line + k
        return pltpu.make_async_remote_copy(
            src_ref=spot, dst_ref=spot, send_sem=w_send.at[i], recv_sem=w_recv.at[i],
            device_id={"seq": line_peer[way]}, device_id_type=MESH,
        )

    def near_copy(array, buffer, stream, way, k, pattern, t):
        spot = block(buffer, stream, way, k, pattern)
        order = low if stream % 2 == 0 else low[::-1]
        i = (((array * size + stream) * 2 + way) * line + k) * near_count + pattern + (1 << t)
        return pltpu.make_async_remote_copy(
            src_ref=spot, dst_ref=spot, send_sem=n_send.at[i], recv_sem=n_recv.at[i],
            device_id={"seq": partner[order[t]]}, device_id_type=MESH,
        )

    def weights(array, buffer, k):
        for stream in range(size):
            for way in (0, 1) if k else (0,):

                def go(stream=stream, way=way):
                    if k:
                        line_copy(array, buffer, stream, way, k, k).wait_recv()
                    if k + 1 < line:
                        for e in (way,) if k else (0, 1):
                            more = place < line - 1 if e == 0 else place > 0
                            when(more, lambda e=e: line_copy(array, buffer, stream, e, k + 1, k).start())
                    for t in range(len(low)):
                        near_copy(array, buffer, stream, way, k, 0, t).start()

                def end(stream=stream, way=way):
                    if k + 1 < line:
                        for e in (way,) if k else (0, 1):
                            more = place < line - 1 if e == 0 else place > 0
                            when(more, lambda e=e: line_copy(array, buffer, stream, e, k + 1, k).wait_send())
                    for t in range(len(low)):
                        near_copy(array, buffer, stream, way, k, 0, t).wait_send()

                when(exists(way, k), go)
                late.append((exists(way, k), end))

    def arrive(array, buffer, k):
        for stream in range(size):
            for way in (0, 1) if k else (0,):

                def go(stream=stream, way=way):
                    for pattern in range(1, near_count):
                        t = pattern.bit_length() - 1
                        near_copy(array, buffer, stream, way, k, pattern - (1 << t), t).wait_recv()
                        for u in range(t + 1, len(low)):
                            near_copy(array, buffer, stream, way, k, pattern, u).start()

                def end(stream=stream, way=way):
                    for pattern in range(1, near_count):
                        for u in range(pattern.bit_length(), len(low)):
                            near_copy(array, buffer, stream, way, k, pattern, u).wait_send()

                when(exists(way, k), go)
                if len(low) > 1:
                    late.append((exists(way, k), end))

    def reduce_gather(parts, stage, landing, full, send_sem, recv_sem, finish):
        held = parts.shape[1]
        base = [0, 0]
        sizes, bases = [], []
        offset = 0
        for step in range(n_bits):
            half = max(held // 2, 1)
            sent = []
            for i in range(2):
                b = reduce_order[i][step]
                if held > 1:
                    away = base[i] + (1 - bit[b]) * half
                    base[i] = base[i] + bit[b] * half
                else:
                    away = base[i]
                source = parts.at[i, pl.ds(away, half)]
                if stage is not None:
                    stage[i, offset : offset + half] = source[...].astype(stage.dtype)
                    source = stage.at[i, pl.ds(offset, half)]
                sent.append(
                    send(
                        source, landing.at[i, pl.ds(offset, half)],
                        send_sem.at[i, step], recv_sem.at[i, step], partner[b],
                    )
                )
            yield
            for i in range(2):
                sent[i].wait_recv()
                if held == 1:
                    sent[i].wait_send()
                    pending[:] = [copy for copy in pending if copy is not sent[i]]
                spot = pl.ds(base[i], half)
                parts[i, spot] = parts[i, spot] + landing[i, offset : offset + half].astype(F32)
            sizes.append((step, half) if held > 1 else None)
            bases.append(list(base))
            offset += half
            held = half
        for i in range(2):
            finish(i, base[i], held)
        for entry in range(n_bits - 1, -1, -1):
            if sizes[entry] is None:
                continue
            step, half = sizes[entry]
            sent = []
            for i in range(2):
                spot = full.at[i, pl.ds(bases[entry][i], half)]
                sent.append(
                    send(
                        spot, spot, send_sem.at[i, n_bits + step], recv_sem.at[i, n_bits + step],
                        partner[reduce_order[i][step]],
                    )
                )
            yield
            for i in range(2):
                sent[i].wait_recv()

    def square_sum():
        have(3)
        sq_in[0] = functools.reduce(jnp.add, [sq[m] for m in range(size)])
        for b in range(n_bits):
            copy = send(sq_in.at[b], sq.at[size + b], sq_send.at[b], sq_recv.at[b], partner[b])
            yield
            copy.wait_recv()
            sq_in[b + 1] = sq_in[b] + sq[size + b]
        inverse[...] = lax.rsqrt(sq_in[n_bits] / text_dim + epsilon)

    def drain(generator, steps=None):
        count = 0
        for _ in generator:
            count += 1
            if steps is not None and count >= steps:
                return

    pieces = sums.shape[1]
    def finish_keys(i, base, held):
        inv = inverse[pl.ds(pl.multiple_of(base * ROWS, ROWS), held * ROWS), :][:, 0:1]
        total = sums[i, pl.ds(base, held)].reshape(held * ROWS, width)
        keys[i, pl.ds(base, held)] = (inv * total).astype(BF16).reshape(held, ROWS, width)

    text_sum = reduce_gather(sums, None, halves, keys, k_send, k_recv, finish_keys)
    norm_sum = square_sum()
    have(4)
    weights(0, wq, 0)
    for i in range(3):
        have(i)
    for i, w in ((0, wk), (1, wv)):
        total = functools.reduce(jnp.add, [dot(st[m], w[m], (1, 0)) for m in range(size)])
        sums[i] = total.reshape(pieces, ROWS, width)

    next(text_sum)
    next(norm_sum)
    have(5)
    weights(1, wo, 0)
    for c in range(cuts):
        move(0, c)
    for p in range(1, line):
        weights(0, wq, p)
        drain(norm_sum, 1)
        if p >= 2:
            drain(text_sum, 1)
        weights(1, wo, p)
        if p == 1:
            for c in range(cuts):
                move(1, c)
        else:
            drain(norm_sum, 1)
            drain(text_sum, 1)
        if p == 2:
            pass_on(0)
    pass_on(1)
    drain(norm_sum)
    for k in range(line):
        arrive(0, wq, k)
    have_rows(0)
    tile = 256 if width % 256 == 0 else 128

    def project(rows, w, out):
        def body(t, _):
            cols = pl.ds(pl.multiple_of(t * tile, tile), tile)
            wide = w[:, :, cols].reshape(-1, tile)
            out[:, cols] = dot(rows[...].reshape(size * toks, -1), wide, (1, 0)).astype(BF16)
            return 0

        lax.fori_loop(0, width // tile, body, 0)

    project(vid, wq, query)
    span = 8 * wq.shape[1]
    tiles = n // 8
    for t in range(tiles):
        wqt[:, t * span : (t + 1) * span] = wq[8 * t : 8 * t + 8].reshape(span, width).T
    drain(text_sum)
    for k in range(line):
        arrive(1, wo, k)
    have_rows(1)
    project(cot, wo, gout)

    scale = HEAD_DIM ** (-0.5)
    text_len = pieces * ROWS

    def attention(h, _):
        cols = pl.ds(pl.multiple_of(h * HEAD_DIM, HEAD_DIM), HEAD_DIM)
        key = keys[0, :, :, cols].reshape(text_len, HEAD_DIM)
        value = keys[1, :, :, cols].reshape(text_len, HEAD_DIM)
        q, g = query[:, cols], gout[:, cols]
        raised = jnp.exp(dot(key, q, (1, 1)) * scale)
        probs = raised * (1.0 / jnp.sum(raised, axis=0, keepdims=True))
        grad_probs = dot(value, g, (1, 1))
        delta = jnp.sum(grad_probs * probs, axis=0, keepdims=True)
        grad_scores = (probs * (grad_probs - delta) * scale).astype(BF16)
        gquery[:, cols] = dot(grad_scores, key, (0, 0)).astype(BF16)
        grads[0, :, :, cols] = dot(grad_scores, q, (1, 0)).reshape(pieces, ROWS, HEAD_DIM)
        grads[1, :, :, cols] = dot(probs.astype(BF16), g, (1, 0)).reshape(pieces, ROWS, HEAD_DIM)
        return 0

    lax.fori_loop(0, width // HEAD_DIM, attention, 0)

    def finish_grads(i, base, held):
        gfull[i, pl.ds(base, held)] = grads[i, pl.ds(base, held)].astype(BF16)

    grad_sum = reduce_gather(grads, gstage, ghalves, gfull, g_send, g_recv, finish_grads)
    next(grad_sum)
    half_rows = chips * toks

    def back(who, t):
        left = gquery[pl.ds(pl.multiple_of(who * half_rows, half_rows), half_rows), :]
        return dot(left, wqt[:, t * span : (t + 1) * span], (1, 0)).reshape(chips, toks, span)

    across, beyond = [], []

    def hand_over(t):
        across[t].wait_recv()
        if chips > 1:
            far_send[t] = (gv_mine[t, 1 - side] + gv_recv[t, 1 - side].astype(F32)).astype(BF16)
            beyond.append(send(far_send.at[t], far_recv.at[t], far_sem.at[t], far_rsem.at[t], mate_device[2]))

    for t in range(tiles):
        gv_send[t] = back(1 - core, t).astype(BF16)
        across.append(send(gv_send.at[t], gv_recv.at[t], gv_sem.at[t], gv_rsem.at[t], sibling))
        gv_mine[t] = back(core, t)
        drain(grad_sum, 1)
        if t > 0:
            hand_over(t - 1)
    hand_over(tiles - 1)
    drain(grad_sum)

    gk, gv = gfull[0].reshape(text_len, width), gfull[1].reshape(text_len, width)
    products = gk.astype(F32) * keys[0].reshape(text_len, width).astype(F32) + gv.astype(F32) * keys[1].reshape(
        text_len, width
    ).astype(F32)
    stat_send[...] = lax.dot_general(
        jnp.ones((8, width), F32), products, (((1,), (1,)), ((), ())),
        precision=lax.Precision.HIGHEST, preferred_element_type=F32,
    )
    ends = []
    for d in range(size - 1, 0, -1):
        tail_send[d - 1] = (dot(gk, wk[mates[d]], (1, 1)) + dot(gv, wv[mates[d]], (1, 1))).astype(BF16)
        ends.append(send(tail_send.at[d - 1], tail_recv.at[d - 1], end_send.at[0, d], end_recv.at[0, d], mate_device[d]))
        ends.append(send(stat_send, stat_recv.at[d - 1], end_send.at[1, d], end_recv.at[1, d], mate_device[d]))
    total = dot(gk, wk[member], (1, 1)) + dot(gv, wv[member], (1, 1))
    for t in range(tiles):
        cols = slice(t * span, (t + 1) * span)
        tile_sum = gv_mine[t, side] + gv_recv[t, side].astype(F32)
        if chips > 1:
            beyond[t].wait_recv()
            tile_sum = tile_sum + far_recv[t].astype(F32)
        grad_video[:, cols] = tile_sum.astype(BF16)
    for copy in ends:
        copy.wait_recv()
    stat = stat_send[...]
    for d in range(1, size):
        total = total + tail_recv[d - 1].astype(F32)
        stat = stat + stat_recv[d - 1]
    grad_normed[...] = total
    row_stat[...] = stat
    for condition, end in late:
        when(condition, end)
    for copy in pending:
        copy.wait_send()


def body(n, heads_split, text_dim, video, cotangent, text_embed, text_gain, w_query, w_key, w_value, w_out):
    toks, model = video.shape
    text_len, feats = text_embed.shape
    rows = w_query.shape[0]
    heads = w_query.shape[1] // HEAD_DIM
    size = 4 if heads % 4 == 0 and n % 4 == 0 else 2
    width = w_query.shape[1] // size
    n_bits = int(math.log2(n // size))
    chips, tiles = size // 2, n // 8
    line = n // size // min(n // size, 4 if size == 2 else 2)
    pieces = text_len // ROWS
    text_wide = text_embed.astype(F32)
    scaled = (text_wide * text_gain).astype(BF16)
    squares = jnp.broadcast_to(jnp.sum(text_wide * text_wide, axis=1, keepdims=True), (text_len, 128))
    lanes = -(-feats // 128) * 128
    if lanes > feats:
        scaled = jnp.pad(scaled, ((0, 0), (0, lanes - feats)))
        w_key, w_value = (jnp.pad(w, ((0, lanes - feats), (0, 0))) for w in (w_key, w_value))
    vmem, dma = pltpu.VMEM, pltpu.SemaphoreType.DMA
    landing = pieces + n_bits
    side = size * toks
    flops = 6 * side * model * width + 10 * side * text_len * width
    out = pl.pallas_call(
        functools.partial(kernel, n, size, text_dim),
        out_shape=[
            jax.ShapeDtypeStruct((toks, model), BF16),
            jax.ShapeDtypeStruct((text_len, lanes), F32),
            jax.ShapeDtypeStruct((8, text_len), F32),
            jax.ShapeDtypeStruct((text_len, 128), F32),
        ],
        in_specs=[pl.BlockSpec(memory_space=pl.ANY)] * 8,
        out_specs=[pl.BlockSpec(memory_space=pltpu.VMEM)] * 4,
        scratch_shapes=[
            vmem((n, rows, width), BF16),
            vmem((n, rows, width), BF16),
            vmem((size, toks, model), BF16),
            vmem((size, toks, model), BF16),
            vmem((size, lanes, width), BF16),
            vmem((size, lanes, width), BF16),
            vmem((size, text_len, lanes), BF16),
            vmem((size + n_bits, text_len, 128), F32),
            vmem((1 + n_bits, text_len, 128), F32),
            vmem((2, pieces, ROWS, width), F32),
            vmem((2, landing, ROWS, width), F32),
            vmem((2, pieces, ROWS, width), BF16),
            vmem((2, pieces, ROWS, width), F32),
            vmem((2, landing, ROWS, width), BF16),
            vmem((2, landing, ROWS, width), BF16),
            vmem((2, pieces, ROWS, width), BF16),
            vmem((side, width), BF16),
            vmem((side, width), BF16),
            vmem((side, width), BF16),
            vmem((width, model), BF16),
            vmem((tiles, chips, toks, model // tiles), BF16),
            vmem((tiles, chips, toks, model // tiles), BF16),
            vmem((tiles, chips, toks, model // tiles), F32),
            vmem((tiles, toks, model // tiles), BF16),
            vmem((tiles, toks, model // tiles), BF16),
            vmem((size - 1, text_len, lanes), BF16),
            vmem((size - 1, text_len, lanes), BF16),
            vmem((8, text_len), F32),
            vmem((size - 1, 8, text_len), F32),
            dma((6, size)),
            dma((6, size)),
            dma((8,)),
            dma((2, 4, 4)),
            dma((2, 4, 4)),
            dma((4 * size * line,)),
            dma((4 * size * line,)),
            dma((4 * n,)),
            dma((4 * n,)),
            dma((n_bits,)),
            dma((n_bits,)),
            dma((2, 2 * n_bits)),
            dma((2, 2 * n_bits)),
            dma((2, 2 * n_bits)),
            dma((2, 2 * n_bits)),
            dma((tiles,)),
            dma((tiles,)),
            dma((tiles,)),
            dma((tiles,)),
            dma((2, size)),
            dma((2, size)),
        ],
        compiler_params=pltpu.CompilerParams(
            collective_id=0, has_side_effects=True, vmem_limit_bytes=63 * 1024 * 1024
        ),
        cost_estimate=pl.CostEstimate(
            flops=flops, bytes_accessed=8 * toks * model, transcendentals=side * text_len * width // HEAD_DIM
        ),
    )(scaled, squares, w_key, w_value, w_query, w_out.T, video, cotangent)
    grad_video, grad_normed, row_stat, inverse = out
    grad_normed = grad_normed[:, 0:feats]
    if heads_split > 1:
        grad_normed, row_stat = lax.psum((grad_normed, row_stat), "head")
        grad_video = lax.psum_scatter(grad_video, "head", scatter_dimension=1, tiled=True)
    inv = inverse[:, 0:1]
    grad_text = inv * (grad_normed * text_gain - text_wide * inv * (row_stat[0][:, None] / text_dim))
    return (grad_video, grad_text)


def solution(mesh):
    n, heads_split = mesh.shape["seq"], mesh.shape["head"]
    in_specs = (
        P("seq", None),
        P("seq", None),
        P(None, "seq"),
        P("seq"),
        P("seq", "head"),
        P("seq", "head"),
        P("seq", "head"),
        P("head", "seq"),
    )
    out_specs = (P("seq", "head"), P(None, "seq"))

    def whole(video, cotangent, text_embed, *rest):
        run = functools.partial(body, n, heads_split, text_embed.shape[1])
        mapped = jax.shard_map(run, mesh=mesh, in_specs=in_specs, out_specs=out_specs, check_vma=False)
        return mapped(video, cotangent, text_embed, *rest)

    return whole
```

```python
import functools
import math

import jax
import jax.numpy as jnp
from jax import lax
from jax.experimental import pallas as pl
from jax.experimental.pallas import tpu as pltpu
from jax.sharding import PartitionSpec as P

HEAD_DIM = 128
ROWS = 16
MESH = pl.DeviceIdType.MESH
epsilon = 1e-06
F32 = jnp.float32
BF16 = jnp.bfloat16


def dot(a, b, dims):
    return lax.dot_general(a, b, ((dims[0:1], dims[1:2]), ((), ())), preferred_element_type=F32)


def kernel(
    n, size, text_dim, scaled, squares, w_key, w_value, w_query, w_out, video, cotangent,
    grad_video, grad_normed, row_stat, inverse,
    wq, wo, vid, cot, wk, wv, st, sq, sq_in,
    sums, halves, keys, grads, gstage, ghalves, gfull, query, gout, gquery, wqt,
    gv_send, gv_recv, gv_mine, far_send, far_recv, tail_send, tail_recv, stat_send, stat_recv,
    pair_send, pair_recv, local_sem, act_send, act_recv, w_send, w_recv, n_send, n_recv, sq_send, sq_recv,
    k_send, k_recv, g_send, g_recv, gv_sem, gv_rsem, far_sem, far_rsem, end_send, end_recv,
):
    me = lax.axis_index("seq")
    group, member = me // size, me % size
    core = me % 2
    sibling = me + 1 - 2 * core
    groups = n // size
    n_bits = int(math.log2(groups))
    bit = [(group // (1 << b)) % 2 for b in range(n_bits)]
    partner = [me + (1 - 2 * bit[b]) * (size << b) for b in range(n_bits)]
    side = member // 2
    mates = []
    for d in range(size):
        mate = member
        if d & 1:
            mate = mate + 1 - 2 * core
        if d & 2:
            mate = mate + 2 - 4 * side
        mates.append(mate)
    mate_device = [group * size + mate for mate in mates]
    near_bits = 2 if size == 2 else 1
    low = list(range(min(near_bits, n_bits)))
    high = list(range(len(low), n_bits))
    reduce_order = [low + high, low[::-1] + high if size == 2 else high + low]
    width = wq.shape[2]
    toks = vid.shape[1]
    pending = []

    line = 1 << len(high)
    near_count = 1 << len(low)
    place = group // near_count
    line_peer = (me + size * near_count, me - size * near_count)
    barrier = pltpu.get_barrier_semaphore()
    peers = mate_device[1:] + partner
    for peer in peers:
        pl.semaphore_signal(barrier, inc=1, device_id={"seq": peer}, device_id_type=MESH)
    for more, peer in ((place < line - 1, line_peer[0]), (place > 0, line_peer[1])):

        @pl.when(more)
        def _():
            pl.semaphore_signal(barrier, inc=1, device_id={"seq": peer}, device_id_type=MESH)

    ends_count = (place + line - 1) // line + (2 * line - 2 - place) // line
    pl.semaphore_wait(barrier, len(peers) + ends_count)

    def send(src, dst, send_sem, recv_sem, peer):
        copy = pltpu.make_async_remote_copy(
            src_ref=src, dst_ref=dst, send_sem=send_sem, recv_sem=recv_sem,
            device_id={"seq": peer}, device_id_type=MESH,
        )
        copy.start()
        pending.append(copy)
        return copy

    def part(array):
        return [array.at[:, pl.ds(pl.multiple_of(mate * width, 128), width)] for mate in mates]

    plan = [
        ([scaled] * size, st.at[member]),
        (part(w_key), wk.at[member]),
        (part(w_value), wv.at[member]),
        ([squares] * size, sq.at[member]),
        (part(w_query), wq.at[me]),
        (part(w_out), wo.at[me]),
    ]
    shared = []
    for i, (sources, dst) in enumerate(plan):
        copies = [
            send(sources[d], dst, pair_send.at[i, d], pair_recv.at[i, d], mate_device[d]) for d in range(1, size)
        ]
        local = pltpu.make_async_copy(sources[0], dst, local_sem.at[i])
        local.start()
        shared.append((copies, local))
    chips = size // 2
    cuts = 4
    piece = toks // cuts
    slots = [(mate % 2) * chips + mate // 2 for mate in mates]
    moving = [[], []]
    own_rows = []
    for i, (rows, buffer) in enumerate(((video, vid), (cotangent, cot))):
        local = pltpu.make_async_copy(rows, buffer.at[slots[0]], local_sem.at[len(plan) + i])
        local.start()
        own_rows.append(local)

    def move(i, c):
        rows, buffer = ((video, vid), (cotangent, cot))[i]
        cut = pl.ds(c * piece, piece)
        dst = buffer.at[slots[0], cut]
        moving[i].append(
            [send(rows.at[cut], dst, act_send.at[i, c, d], act_recv.at[i, c, d], mate_device[d]) for d in range(min(size, 3) - 1, 0, -1)]
        )

    def have(i):
        for copy in shared[i][0]:
            copy.wait_recv()
        shared[i][1].wait()

    def pass_on(i):
        if size > 2:
            for c in range(cuts):
                copies = moving[i][c]
                copies[0].wait_recv()
                rows = (vid, cot)[i].at[slots[2], pl.ds(c * piece, piece)]
                copies.append(send(rows, rows, act_send.at[i, c, 3], act_recv.at[i, c, 3], mate_device[1]))

    def have_rows(i):
        for copies in moving[i]:
            for copy in copies[1:] if size > 2 else copies:
                copy.wait_recv()
        own_rows[i].wait()

    late = []

    def when(condition, run):
        if condition is None:
            run()
        else:
            pl.when(condition)(run)

    def exists(way, k):
        if k == 0:
            return None
        return place >= k if way == 0 else place < line - k

    def block(buffer, stream, way, k, pattern=0):
        where = group + (k if way else -k) * near_count
        order = low if stream % 2 == 0 else low[::-1]
        for t in range(len(low)):
            if (pattern >> t) & 1:
                where = where + (1 - 2 * bit[order[t]]) * (1 << order[t])
        return buffer.at[size * where + stream]

    def line_copy(array, buffer, stream, way, k, at):
        spot = block(buffer, stream, way, at)
        i = ((array * size + stream) * 2 + way) * line + k
        return pltpu.make_async_remote_copy(
            src_ref=spot, dst_ref=spot, send_sem=w_send.at[i], recv_sem=w_recv.at[i],
            device_id={"seq": line_peer[way]}, device_id_type=MESH,
        )

    def near_copy(array, buffer, stream, way, k, pattern, t):
        spot = block(buffer, stream, way, k, pattern)
        order = low if stream % 2 == 0 else low[::-1]
        i = (((array * size + stream) * 2 + way) * line + k) * near_count + pattern + (1 << t)
        return pltpu.make_async_remote_copy(
            src_ref=spot, dst_ref=spot, send_sem=n_send.at[i], recv_sem=n_recv.at[i],
            device_id={"seq": partner[order[t]]}, device_id_type=MESH,
        )

    def weights(array, buffer, k):
        for stream in range(size):
            for way in (0, 1) if k else (0,):

                def go(stream=stream, way=way):
                    if k:
                        line_copy(array, buffer, stream, way, k, k).wait_recv()
                    if k + 1 < line:
                        for e in (way,) if k else (0, 1):
                            more = place < line - 1 if e == 0 else place > 0
                            when(more, lambda e=e: line_copy(array, buffer, stream, e, k + 1, k).start())
                    for t in range(len(low)):
                        near_copy(array, buffer, stream, way, k, 0, t).start()

                def end(stream=stream, way=way):
                    if k + 1 < line:
                        for e in (way,) if k else (0, 1):
                            more = place < line - 1 if e == 0 else place > 0
                            when(more, lambda e=e: line_copy(array, buffer, stream, e, k + 1, k).wait_send())
                    for t in range(len(low)):
                        near_copy(array, buffer, stream, way, k, 0, t).wait_send()

                when(exists(way, k), go)
                late.append((exists(way, k), end))

    def arrive(array, buffer, k):
        for stream in range(size):
            for way in (0, 1) if k else (0,):

                def go(stream=stream, way=way):
                    for pattern in range(1, near_count):
                        t = pattern.bit_length() - 1
                        near_copy(array, buffer, stream, way, k, pattern - (1 << t), t).wait_recv()
                        for u in range(t + 1, len(low)):
                            near_copy(array, buffer, stream, way, k, pattern, u).start()

                def end(stream=stream, way=way):
                    for pattern in range(1, near_count):
                        for u in range(pattern.bit_length(), len(low)):
                            near_copy(array, buffer, stream, way, k, pattern, u).wait_send()

                when(exists(way, k), go)
                if len(low) > 1:
                    late.append((exists(way, k), end))

    def reduce_gather(parts, stage, landing, full, send_sem, recv_sem, finish):
        held = parts.shape[1]
        base = [0, 0]
        sizes, bases = [], []
        offset = 0
        for step in range(n_bits):
            half = max(held // 2, 1)
            sent = []
            for i in range(2):
                b = reduce_order[i][step]
                if held > 1:
                    away = base[i] + (1 - bit[b]) * half
                    base[i] = base[i] + bit[b] * half
                else:
                    away = base[i]
                source = parts.at[i, pl.ds(away, half)]
                if stage is not None:
                    stage[i, offset : offset + half] = source[...].astype(stage.dtype)
                    source = stage.at[i, pl.ds(offset, half)]
                sent.append(
                    send(
                        source, landing.at[i, pl.ds(offset, half)],
                        send_sem.at[i, step], recv_sem.at[i, step], partner[b],
                    )
                )
            yield
            for i in range(2):
                sent[i].wait_recv()
                if held == 1:
                    sent[i].wait_send()
                    pending[:] = [copy for copy in pending if copy is not sent[i]]
                spot = pl.ds(base[i], half)
                parts[i, spot] = parts[i, spot] + landing[i, offset : offset + half].astype(F32)
            sizes.append((step, half) if held > 1 else None)
            bases.append(list(base))
            offset += half
            held = half
        for i in range(2):
            finish(i, base[i], held)
        for entry in range(n_bits - 1, -1, -1):
            if sizes[entry] is None:
                continue
            step, half = sizes[entry]
            sent = []
            for i in range(2):
                spot = full.at[i, pl.ds(bases[entry][i], half)]
                sent.append(
                    send(
                        spot, spot, send_sem.at[i, n_bits + step], recv_sem.at[i, n_bits + step],
                        partner[reduce_order[i][step]],
                    )
                )
            yield
            for i in range(2):
                sent[i].wait_recv()

    def square_sum():
        have(3)
        sq_in[0] = functools.reduce(jnp.add, [sq[m] for m in range(size)])
        for b in range(n_bits):
            copy = send(sq_in.at[b], sq.at[size + b], sq_send.at[b], sq_recv.at[b], partner[b])
            yield
            copy.wait_recv()
            sq_in[b + 1] = sq_in[b] + sq[size + b]
        inverse[...] = lax.rsqrt(sq_in[n_bits] / text_dim + epsilon)

    def drain(generator, steps=None):
        count = 0
        for _ in generator:
            count += 1
            if steps is not None and count >= steps:
                return

    pieces = sums.shape[1]
    def finish_keys(i, base, held):
        inv = inverse[pl.ds(pl.multiple_of(base * ROWS, ROWS), held * ROWS), :][:, 0:1]
        total = sums[i, pl.ds(base, held)].reshape(held * ROWS, width)
        keys[i, pl.ds(base, held)] = (inv * total).astype(BF16).reshape(held, ROWS, width)

    text_sum = reduce_gather(sums, None, halves, keys, k_send, k_recv, finish_keys)
    norm_sum = square_sum()
    have(4)
    weights(0, wq, 0)
    for i in range(3):
        have(i)
    for i, w in ((0, wk), (1, wv)):
        total = functools.reduce(jnp.add, [dot(st[m], w[m], (1, 0)) for m in range(size)])
        sums[i] = total.reshape(pieces, ROWS, width)

    next(text_sum)
    next(norm_sum)
    have(5)
    weights(1, wo, 0)
    for c in range(cuts):
        move(0, c)
    for p in range(1, line):
        weights(0, wq, p)
        drain(norm_sum, 1)
        if p >= 2:
            drain(text_sum, 1)
        weights(1, wo, p)
        if p == 1:
            for c in range(cuts):
                move(1, c)
        else:
            drain(norm_sum, 1)
            drain(text_sum, 1)
        if p == 2:
            pass_on(0)
    pass_on(1)
    drain(norm_sum)
    for k in range(line):
        arrive(0, wq, k)
    have_rows(0)
    tile = 256 if width % 256 == 0 else 128

    def project(rows, w, out):
        def body(t, _):
            cols = pl.ds(pl.multiple_of(t * tile, tile), tile)
            wide = w[:, :, cols].reshape(-1, tile)
            out[:, cols] = dot(rows[...].reshape(size * toks, -1), wide, (1, 0)).astype(BF16)
            return 0

        lax.fori_loop(0, width // tile, body, 0)

    project(vid, wq, query)
    span = 8 * wq.shape[1]
    tiles = n // 8
    for t in range(tiles):
        wqt[:, t * span : (t + 1) * span] = wq[8 * t : 8 * t + 8].reshape(span, width).T
    drain(text_sum)
    for k in range(line):
        arrive(1, wo, k)
    have_rows(1)
    project(cot, wo, gout)

    scale = HEAD_DIM ** (-0.5)
    text_len = pieces * ROWS

    def slot_rows(slot):
        return pl.ds(pl.multiple_of(slot * toks, toks), toks)

    def attend(x, more):
        def attention(h, _):
            cols = pl.ds(pl.multiple_of(h * HEAD_DIM, HEAD_DIM), HEAD_DIM)
            key = keys[0, :, :, cols].reshape(text_len, HEAD_DIM)
            value = keys[1, :, :, cols].reshape(text_len, HEAD_DIM)
            gk, gv = 0.0, 0.0
            for c in range(2):
                rows = slot_rows(c * chips + x)
                q, g = query[rows, cols], gout[rows, cols]
                raised = jnp.exp(dot(key, q, (1, 1)) * scale)
                probs = raised * (1.0 / jnp.sum(raised, axis=0, keepdims=True))
                grad_probs = dot(value, g, (1, 1))
                delta = jnp.sum(grad_probs * probs, axis=0, keepdims=True)
                grad_scores = (probs * (grad_probs - delta) * scale).astype(BF16)
                gquery[rows, cols] = dot(grad_scores, key, (0, 0)).astype(BF16)
                gk = gk + dot(grad_scores, q, (1, 0))
                gv = gv + dot(probs.astype(BF16), g, (1, 0))
            gk, gv = gk.reshape(pieces, ROWS, HEAD_DIM), gv.reshape(pieces, ROWS, HEAD_DIM)
            grads[0, :, :, cols] = grads[0, :, :, cols] + gk if more else gk
            grads[1, :, :, cols] = grads[1, :, :, cols] + gv if more else gv
            return 0

        lax.fori_loop(0, width // HEAD_DIM, attention, 0)

    def finish_grads(i, base, held):
        gfull[i, pl.ds(base, held)] = grads[i, pl.ds(base, held)].astype(BF16)


    def back(slot, t):
        return dot(gquery[slot_rows(slot), :], wqt[:, t * span : (t + 1) * span], (1, 0))

    def across_cores(x, place, t):
        gv_send[t, place] = back((1 - core) * chips + x, t).astype(BF16)
        return send(
            gv_send.at[t, place], gv_recv.at[t, place], gv_sem.at[t, place], gv_rsem.at[t, place], sibling
        )

    beyond = []
    if chips > 1:
        attend(1 - side, False)
        across = []

        def hand_over(t):
            across[t].wait_recv()
            far_send[t] = (gv_mine[t, 1] + gv_recv[t, 1].astype(F32)).astype(BF16)
            beyond.append(send(far_send.at[t], far_recv.at[t], far_sem.at[t], far_rsem.at[t], mate_device[2]))

        for t in range(tiles):
            across.append(across_cores(1 - side, 1, t))
            gv_mine[t, 1] = back(core * chips + 1 - side, t)
            if t > 0:
                hand_over(t - 1)
        hand_over(tiles - 1)
    attend(side, chips > 1)
    grad_sum = reduce_gather(grads, gstage, ghalves, gfull, g_send, g_recv, finish_grads)
    next(grad_sum)
    near_copies = []
    for t in range(tiles):
        near_copies.append(across_cores(side, 0, t))
        gv_mine[t, 0] = back(core * chips + side, t)
        drain(grad_sum, 1)
    drain(grad_sum)

    gk, gv = gfull[0].reshape(text_len, width), gfull[1].reshape(text_len, width)
    products = gk.astype(F32) * keys[0].reshape(text_len, width).astype(F32) + gv.astype(F32) * keys[1].reshape(
        text_len, width
    ).astype(F32)
    stat_send[...] = lax.dot_general(
        jnp.ones((8, width), F32), products, (((1,), (1,)), ((), ())),
        precision=lax.Precision.HIGHEST, preferred_element_type=F32,
    )
    ends = []
    for d in range(size - 1, 0, -1):
        tail_send[d - 1] = (dot(gk, wk[mates[d]], (1, 1)) + dot(gv, wv[mates[d]], (1, 1))).astype(BF16)
        ends.append(send(tail_send.at[d - 1], tail_recv.at[d - 1], end_send.at[0, d], end_recv.at[0, d], mate_device[d]))
        ends.append(send(stat_send, stat_recv.at[d - 1], end_send.at[1, d], end_recv.at[1, d], mate_device[d]))
    total = dot(gk, wk[member], (1, 1)) + dot(gv, wv[member], (1, 1))
    for t in range(tiles):
        cols = slice(t * span, (t + 1) * span)
        near_copies[t].wait_recv()
        tile_sum = gv_mine[t, 0] + gv_recv[t, 0].astype(F32)
        if chips > 1:
            beyond[t].wait_recv()
            tile_sum = tile_sum + far_recv[t].astype(F32)
        grad_video[:, cols] = tile_sum.astype(BF16)
    for copy in ends:
        copy.wait_recv()
    stat = stat_send[...]
    for d in range(1, size):
        total = total + tail_recv[d - 1].astype(F32)
        stat = stat + stat_recv[d - 1]
    grad_normed[...] = total
    row_stat[...] = stat
    for condition, end in late:
        when(condition, end)
    for copy in pending:
        copy.wait_send()


def body(n, heads_split, text_dim, video, cotangent, text_embed, text_gain, w_query, w_key, w_value, w_out):
    toks, model = video.shape
    text_len, feats = text_embed.shape
    rows = w_query.shape[0]
    heads = w_query.shape[1] // HEAD_DIM
    size = 4 if heads % 4 == 0 and n % 4 == 0 else 2
    width = w_query.shape[1] // size
    n_bits = int(math.log2(n // size))
    chips, tiles = size // 2, n // 8
    line = n // size // min(n // size, 4 if size == 2 else 2)
    pieces = text_len // ROWS
    text_wide = text_embed.astype(F32)
    scaled = (text_wide * text_gain).astype(BF16)
    squares = jnp.broadcast_to(jnp.sum(text_wide * text_wide, axis=1, keepdims=True), (text_len, 128))
    lanes = -(-feats // 128) * 128
    if lanes > feats:
        scaled = jnp.pad(scaled, ((0, 0), (0, lanes - feats)))
        w_key, w_value = (jnp.pad(w, ((0, lanes - feats), (0, 0))) for w in (w_key, w_value))
    vmem, dma = pltpu.VMEM, pltpu.SemaphoreType.DMA
    landing = pieces + n_bits
    side = size * toks
    flops = 6 * side * model * width + 10 * side * text_len * width
    out = pl.pallas_call(
        functools.partial(kernel, n, size, text_dim),
        out_shape=[
            jax.ShapeDtypeStruct((toks, model), BF16),
            jax.ShapeDtypeStruct((text_len, lanes), F32),
            jax.ShapeDtypeStruct((8, text_len), F32),
            jax.ShapeDtypeStruct((text_len, 128), F32),
        ],
        in_specs=[pl.BlockSpec(memory_space=pl.ANY)] * 8,
        out_specs=[pl.BlockSpec(memory_space=pltpu.VMEM)] * 4,
        scratch_shapes=[
            vmem((n, rows, width), BF16),
            vmem((n, rows, width), BF16),
            vmem((size, toks, model), BF16),
            vmem((size, toks, model), BF16),
            vmem((size, lanes, width), BF16),
            vmem((size, lanes, width), BF16),
            vmem((size, text_len, lanes), BF16),
            vmem((size + n_bits, text_len, 128), F32),
            vmem((1 + n_bits, text_len, 128), F32),
            vmem((2, pieces, ROWS, width), F32),
            vmem((2, landing, ROWS, width), F32),
            vmem((2, pieces, ROWS, width), BF16),
            vmem((2, pieces, ROWS, width), F32),
            vmem((2, landing, ROWS, width), BF16),
            vmem((2, landing, ROWS, width), BF16),
            vmem((2, pieces, ROWS, width), BF16),
            vmem((side, width), BF16),
            vmem((side, width), BF16),
            vmem((side, width), BF16),
            vmem((width, model), BF16),
            vmem((tiles, chips, toks, model // tiles), BF16),
            vmem((tiles, chips, toks, model // tiles), BF16),
            vmem((tiles, chips, toks, model // tiles), F32),
            vmem((tiles, toks, model // tiles), BF16),
            vmem((tiles, toks, model // tiles), BF16),
            vmem((size - 1, text_len, lanes), BF16),
            vmem((size - 1, text_len, lanes), BF16),
            vmem((8, text_len), F32),
            vmem((size - 1, 8, text_len), F32),
            dma((6, size)),
            dma((6, size)),
            dma((8,)),
            dma((2, 4, 4)),
            dma((2, 4, 4)),
            dma((4 * size * line,)),
            dma((4 * size * line,)),
            dma((4 * n,)),
            dma((4 * n,)),
            dma((n_bits,)),
            dma((n_bits,)),
            dma((2, 2 * n_bits)),
            dma((2, 2 * n_bits)),
            dma((2, 2 * n_bits)),
            dma((2, 2 * n_bits)),
            dma((tiles, 2)),
            dma((tiles, 2)),
            dma((tiles,)),
            dma((tiles,)),
            dma((2, size)),
            dma((2, size)),
        ],
        compiler_params=pltpu.CompilerParams(
            collective_id=0, has_side_effects=True, vmem_limit_bytes=63 * 1024 * 1024
        ),
        cost_estimate=pl.CostEstimate(
            flops=flops, bytes_accessed=8 * toks * model, transcendentals=side * text_len * width // HEAD_DIM
        ),
    )(scaled, squares, w_key, w_value, w_query, w_out.T, video, cotangent)
    grad_video, grad_normed, row_stat, inverse = out
    grad_normed = grad_normed[:, 0:feats]
    if heads_split > 1:
        grad_normed, row_stat = lax.psum((grad_normed, row_stat), "head")
        grad_video = lax.psum_scatter(grad_video, "head", scatter_dimension=1, tiled=True)
    inv = inverse[:, 0:1]
    grad_text = inv * (grad_normed * text_gain - text_wide * inv * (row_stat[0][:, None] / text_dim))
    return (grad_video, grad_text)


def solution(mesh):
    n, heads_split = mesh.shape["seq"], mesh.shape["head"]
    in_specs = (
        P("seq", None),
        P("seq", None),
        P(None, "seq"),
        P("seq"),
        P("seq", "head"),
        P("seq", "head"),
        P("seq", "head"),
        P("head", "seq"),
    )
    out_specs = (P("seq", "head"), P(None, "seq"))

    def whole(video, cotangent, text_embed, *rest):
        run = functools.partial(body, n, heads_split, text_embed.shape[1])
        mapped = jax.shard_map(run, mesh=mesh, in_specs=in_specs, out_specs=out_specs, check_vma=False)
        return mapped(video, cotangent, text_embed, *rest)

    return whole
```
